256 devices in a mesh: grp: 4 (over y), stretch: 64 (over z, x, core).
Axes of the slice: x: 4, y: 4, z: 8, core: 2. Of those that a mesh axis runs over, the one named last changes fastest.
Arguments:
- queries: bfloat16 [131072, 512], P(('grp', 'stretch')), may hold values from -6 to 6
- keys: bfloat16 [131072, 512], P(('grp', 'stretch')), may hold values from -6 to 6
- values: bfloat16 [131072, 512], P(('grp', 'stretch')), may hold values from -6 to 6
- grad_out: bfloat16 [131072, 512], P(('grp', 'stretch')), may hold values from -6 to 6
- positions: int32 [131072], P(('grp', 'stretch')), may hold values from 0 to 8191, as said below
Outputs:
- grad_queries: bfloat16 [131072, 512], P(('grp', 'stretch'))
- grad_keys: bfloat16 [131072, 512], P(('grp', 'stretch'))
- grad_values: bfloat16 [131072, 512], P(('grp', 'stretch'))
The draws below stay inside these ranges and needn't reach their ends.
Inputs may be any that keep to these rules, and one draw needn't show every extreme that they name: `positions`: each position is 0 or one more than the position of the token before it; the first token has position 0; no document is longer than min(65536, 8192) tokens, and the last document is exactly that long.
All inputs are finite; a program needn't handle non-finite values.
Results may differ from the reference program's by a relative error of at most 0.006.
Values sent between devices are 32-bit elements; how exact they have to be, the bound alone decides.
No kernel may reach another device: no remote copies, remote signals or barrier semaphores. Data moves between devices by JAX's collectives and lax.ppermute only.
A program may use at most 256 MiB of HBM per device.

```python
import math
import jax
import jax.numpy as jnp
from jax import lax

HEADS = 4
HEAD_DIM = 128
BLOCK = 512
WIDTH = 512
TOKENS = 131072


span_limit = 8192


def draw_positions(key, part):
    key = jax.random.fold_in(key, 11)
    last_span = min(TOKENS // 2, span_limit)
    last_start = TOKENS - last_span
    marks = jax.random.randint(key, (TOKENS,), 0, 32)
    index = jnp.arange(TOKENS, dtype=jnp.int32)
    early = index < last_start
    forced = (index % span_limit == 0) & early | (index == last_start)
    random_start = (marks == 0) & early
    starts = jnp.where(forced | random_start, index, 0)
    return (index - lax.cummax(starts, axis=0)).astype(jnp.int32)


def steps_of(rng, extent, cuts, smallest, largest):
    gain = 1.0
    for dim, shards_of in cuts:
        heights = jax.random.uniform(jax.random.fold_in(jax.random.fold_in(rng, 6), dim), (shards_of,), jnp.float32, smallest / len(cuts), largest / len(cuts))
        gain = gain * jnp.repeat(jnp.exp(heights), extent[dim] // shards_of).reshape((-1,) + (1,) * (len(extent) - 1 - dim))
    return gain


def scatter_about(stream_key, extent, scale, bound, pieces=(), kind=jnp.bfloat16):
    loudness = steps_of(stream_key, extent, pieces, -0.22, 0.18) if pieces else 1.0
    drawn = jax.random.normal(stream_key, extent, jnp.float32) * scale * loudness
    return jnp.minimum(jnp.maximum(drawn, -bound), bound).astype(kind)


def setup_inputs(seed: int = 0) -> dict:
    seeds = jax.random.split(jax.random.key(seed), 6)
    queries = scatter_about(seeds[0], (TOKENS, WIDTH), 1.0, 6.0, ((0, 256),))
    keys = scatter_about(seeds[1], (TOKENS, WIDTH), 1.0, 6.0, ((0, 256),))
    values = scatter_about(seeds[2], (TOKENS, WIDTH), 1.0, 6.0, ((0, 256),))
    grad_out = scatter_about(seeds[3], (TOKENS, WIDTH), 1.0, 6.0, ((0, 256),))
    positions = draw_positions(jax.random.fold_in(seeds[5], 71), 0)
    return dict(queries=queries, keys=keys, values=values, grad_out=grad_out, positions=positions)


THETA = 500000.0

def rotary_tables(positions, heads, head_dim):
    half_dim = head_dim // 2
    steps_j = jnp.arange(half_dim, dtype=jnp.float32)
    frequency = jnp.power(jnp.asarray(THETA, jnp.float32), -2.0 * steps_j / head_dim)
    angles = positions.astype(jnp.float32)[:, None] * frequency[None, :]
    cosine = jnp.tile(jnp.cos(angles), (1, 2 * heads))
    sine = jnp.tile(jnp.sin(angles), (1, 2 * heads))
    return (cosine, sine)

def rotate_rows(rows, cosine, sine, heads, head_dim):
    wide = rows.astype(jnp.float32)
    split = wide.reshape(wide.shape[0], heads, 2, head_dim // 2)
    turned = jnp.concatenate([-split[:, :, 1:], split[:, :, :1]], axis=2).reshape(wide.shape)
    return wide * cosine + turned * sine

def unrotate_rows(grads, cosine, sine, heads, head_dim):
    scaled = grads * sine
    split = scaled.reshape(grads.shape[0], heads, 2, head_dim // 2)
    turned = jnp.concatenate([split[:, :, 1:], -split[:, :, :1]], axis=2).reshape(grads.shape)
    return grads * cosine + turned

def reference(queries, keys, values, grad_out, positions):
    scale = 1.0 / math.sqrt(HEAD_DIM * TOKENS)
    count = TOKENS // BLOCK
    width = HEADS * HEAD_DIM
    f32 = jnp.float32
    q_blocks = queries.reshape(count, BLOCK, width)
    k_blocks = keys.reshape(count, BLOCK, width)
    v_blocks = values.reshape(count, BLOCK, width)
    o_blocks = grad_out.reshape(count, BLOCK, width)
    p_blocks = positions.reshape(count, BLOCK)

    def states(items):
        q_one, k_one, v_one, o_one, p_one = items
        cosine, sine = rotary_tables(p_one, HEADS, HEAD_DIM)
        q_rot = rotate_rows(q_one, cosine, sine, HEADS, HEAD_DIM).astype(jnp.bfloat16)
        k_rot = rotate_rows(k_one, cosine, sine, HEADS, HEAD_DIM).astype(jnp.bfloat16)
        shape3 = (BLOCK, HEADS, HEAD_DIM)
        key_state = jnp.einsum('shd,she->hde', k_rot.reshape(shape3).astype(f32), v_one.reshape(shape3).astype(f32))
        query_state = jnp.einsum('thd,the->hde', q_rot.reshape(shape3).astype(f32), o_one.reshape(shape3).astype(f32))
        return (key_state, query_state)
    key_states, query_states = lax.map(states, (q_blocks, k_blocks, v_blocks, o_blocks, p_blocks))
    zero_state = jnp.zeros((1, HEADS, HEAD_DIM, HEAD_DIM), f32)
    prior = jnp.concatenate([zero_state, jnp.cumsum(key_states, axis=0)[:-1]], axis=0)
    later = jnp.concatenate([jnp.cumsum(query_states[::-1], axis=0)[::-1][1:], zero_state], axis=0)
    prior_bf = (scale * prior).astype(jnp.bfloat16)
    later_bf = (scale * later).astype(jnp.bfloat16)
    lower = jnp.arange(BLOCK)[:, None] >= jnp.arange(BLOCK)[None, :]
    upper = jnp.arange(BLOCK)[:, None] <= jnp.arange(BLOCK)[None, :]

    def kernel(items):
        q_one, k_one, v_one, o_one, p_one, prior_one, later_one = items
        cosine, sine = rotary_tables(p_one, HEADS, HEAD_DIM)
        shape3 = (BLOCK, HEADS, HEAD_DIM)
        q_rot = rotate_rows(q_one, cosine, sine, HEADS, HEAD_DIM).astype(jnp.bfloat16).reshape(shape3).astype(f32)
        k_rot = rotate_rows(k_one, cosine, sine, HEADS, HEAD_DIM).astype(jnp.bfloat16).reshape(shape3).astype(f32)
        v_three = v_one.reshape(shape3).astype(f32)
        o_three = o_one.reshape(shape3).astype(f32)
        weights_p = jnp.where(lower[None], scale * jnp.einsum('thd,shd->hts', o_three, v_three), 0.0).astype(jnp.bfloat16).astype(f32)
        weights_r = jnp.where(upper[None], scale * jnp.einsum('shd,thd->hst', k_rot, q_rot), 0.0).astype(jnp.bfloat16).astype(f32)
        prior_f = prior_one.astype(f32)
        later_f = later_one.astype(f32)
        dq_rot = jnp.einsum('hts,shd->thd', weights_p, k_rot) + jnp.einsum('the,hde->thd', o_three, prior_f)
        dk_rot = jnp.einsum('hts,thd->shd', weights_p, q_rot) + jnp.einsum('she,hde->shd', v_three, later_f)
        dv_all = jnp.einsum('hst,the->she', weights_r, o_three) + jnp.einsum('shd,hde->she', k_rot, later_f)
        grad_q = unrotate_rows(dq_rot.reshape(BLOCK, width), cosine, sine, HEADS, HEAD_DIM).astype(jnp.bfloat16)
        grad_k = unrotate_rows(dk_rot.reshape(BLOCK, width), cosine, sine, HEADS, HEAD_DIM).astype(jnp.bfloat16)
        return (grad_q, grad_k, dv_all.reshape(BLOCK, width).astype(jnp.bfloat16))
    grad_q, grad_k, grad_v = lax.map(kernel, (q_blocks, k_blocks, v_blocks, o_blocks, p_blocks, prior_bf, later_bf))
    return (grad_q.reshape(TOKENS, width), grad_k.reshape(TOKENS, width), grad_v.reshape(TOKENS, width))
```

```python
import math

import numpy as np
import jax
import jax.numpy as jnp
from jax import lax
from jax.experimental import pallas as pl
from jax.experimental.pallas import tpu as pltpu
from jax.sharding import Mesh, PartitionSpec as P

HEADS = 4
HEAD_DIM = 128
BLOCK = 512
THETA = 500000.0
WIDTH = HEADS * HEAD_DIM
HALF = HEAD_DIM // 2
F32 = jnp.float32
BF16 = jnp.bfloat16
VMEM_LIMIT = 48 * 1024 * 1024
WHOLE = pl.BlockSpec(memory_space=pltpu.VMEM)
SCALAR = pl.BlockSpec(memory_space=pltpu.SMEM)

FREQUENCY = np.tile(
    np.power(THETA, -2.0 * np.arange(HALF) / HEAD_DIM), 2
).astype(np.float32)[None, :]

HALF_PI = (1.5703125, 4.837512969970703125e-4, 7.54978995489188216e-8)


def params():
    return pltpu.CompilerParams(vmem_limit_bytes=VMEM_LIMIT)


def sin_cos(angle):
    turns = jnp.floor(angle * (2.0 / math.pi) + 0.5)
    r = angle - turns * HALF_PI[0]
    r = r - turns * HALF_PI[1]
    r = r - turns * HALF_PI[2]
    r2 = r * r
    s = r + r * r2 * (-1.6666654611e-1 + r2 * (8.3321608736e-3 + r2 * -1.9515295891e-4))
    c = 1.0 + r2 * (-0.5 + r2 * (4.166664568298827e-2 + r2 * (-1.388731625493765e-3 + r2 * 2.443315711809948e-5)))
    quadrant = turns.astype(jnp.int32) & 3
    odd = (quadrant & 1) == 1
    sine = jnp.where(odd, c, s)
    cosine = jnp.where(odd, s, c)
    sine = jnp.where(quadrant >= 2, -sine, sine)
    cosine = jnp.where((quadrant == 1) | (quadrant == 2), -cosine, cosine)
    return sine, cosine


def dot(a, b, dims):
    return lax.dot_general(a, b, (dims, ((), ())), preferred_element_type=F32)


def head(ref, h):
    return ref[:, h * HEAD_DIM : (h + 1) * HEAD_DIM]


def rotate_kernel(core_ref, pos_ref, freq_ref, q_ref, k_ref, v_ref, o_ref, qr_ref, kr_ref, cos_ref, sin_ref, mine_ref, other_ref):
    core = core_ref[0]
    first = lax.broadcasted_iota(jnp.int32, (HEAD_DIM, HEAD_DIM), 1) < HALF
    for i in range(BLOCK // HEAD_DIM):
        row = jnp.broadcast_to(pos_ref[i : i + 1, :].astype(F32), (HEAD_DIM, HEAD_DIM))
        sine, cosine = sin_cos(row.T * freq_ref[...])
        rows = slice(i * HEAD_DIM, (i + 1) * HEAD_DIM)
        cos_ref[rows, :] = cosine
        sin_ref[rows, :] = jnp.where(first, -sine, sine)
    for h in range(HEADS):
        cosine, sine = cos_ref[...], sin_ref[...]
        cols = slice(h * HEAD_DIM, (h + 1) * HEAD_DIM)
        q = head(q_ref, h).astype(F32)
        qr = (q * cosine + pltpu.roll(q, HALF, 1) * sine).astype(BF16)
        qr_ref[:, cols] = qr
        k = head(k_ref, h).astype(F32)
        kr = (k * cosine + pltpu.roll(k, HALF, 1) * sine).astype(BF16)
        kr_ref[:, cols] = kr
        key_state = dot(kr, head(v_ref, h), ((0,), (0,)))
        query_state = dot(qr, head(o_ref, h), ((0,), (0,)))
        rows = slice(h * HEAD_DIM, (h + 1) * HEAD_DIM)
        mine_ref[rows, :] = jnp.where(core == 0, key_state, query_state)
        other_ref[rows, :] = jnp.where(core == 0, query_state, key_state)


def intra_kernel(qr_ref, kr_ref, v_ref, o_ref, dq_ref, dk_ref, dv_ref):
    n = BLOCK // 2
    row = lax.broadcasted_iota(jnp.int32, (n, n), 0)
    col = lax.broadcasted_iota(jnp.int32, (n, n), 1)
    lower = row >= col
    upper = row <= col
    top, low = slice(0, n), slice(n, BLOCK)
    lanes = ((1,), (1,))
    plain = ((1,), (0,))
    for h in range(HEADS):
        cols = slice(h * HEAD_DIM, (h + 1) * HEAD_DIM)
        q1, q2 = qr_ref[top, cols], qr_ref[low, cols]
        k1, k2 = kr_ref[top, cols], kr_ref[low, cols]
        v1, v2 = v_ref[top, cols], v_ref[low, cols]
        o1, o2 = o_ref[top, cols], o_ref[low, cols]

        def score(a, b, mask=None):
            s = dot(a, b, lanes)
            return (s if mask is None else jnp.where(mask, s, 0.0)).astype(BF16)

        dq_ref[top, cols] = dot(score(o1, v1, lower), k1, plain)
        dq_ref[low, cols] = dot(score(o2, v1), k1, plain) + dot(score(o2, v2, lower), k2, plain)
        dk_ref[top, cols] = dot(score(v1, o1, upper), q1, plain) + dot(score(v1, o2), q2, plain)
        dk_ref[low, cols] = dot(score(v2, o2, upper), q2, plain)
        dv_ref[top, cols] = dot(score(k1, q1, upper), o1, plain) + dot(score(k1, q2), o2, plain)
        dv_ref[low, cols] = dot(score(k2, q2, upper), o2, plain)


def scan_kernel(core_ref, r_ref, total_ref, pre_ref):
    n = r_ref.shape[0]
    total = r_ref[0]
    for i in range(1, n):
        total = total + r_ref[i]
    total_ref[...] = total
    up = core_ref[0] == 0

    @pl.when(up)
    def _():
        acc = jnp.zeros_like(total)
        for i in range(n):
            pre_ref[i] = acc
            acc = acc + r_ref[i]

    @pl.when(jnp.logical_not(up))
    def _():
        acc = jnp.zeros_like(total)
        for i in reversed(range(n)):
            pre_ref[i] = acc
            acc = acc + r_ref[i]


def final_kernel(core_ref, chip_ref, recv_ref, kr_ref, v_ref, o_ref, cos_ref, sin_ref, dq_ref, dk_ref, dv_ref, gq_ref, gk_ref, gv_ref, *, scale):
    core = core_ref[0]
    cosine = cos_ref[...] * scale
    sine = sin_ref[...] * scale
    for h in range(HEADS):
        cols = slice(h * HEAD_DIM, (h + 1) * HEAD_DIM)
        rows = slice(h * HEAD_DIM, (h + 1) * HEAD_DIM)
        chip, recv = chip_ref[rows, :], recv_ref[rows, :]
        prior = jnp.where(core == 0, chip, recv).astype(BF16)
        later = jnp.where(core == 0, recv, chip).astype(BF16)
        dq = dq_ref[:, cols] + dot(o_ref[:, cols], prior, ((1,), (1,)))
        gq_ref[:, cols] = (dq * cosine - pltpu.roll(dq, HALF, 1) * sine).astype(BF16)
        dk = dk_ref[:, cols] + dot(v_ref[:, cols], later, ((1,), (1,)))
        gk_ref[:, cols] = (dk * cosine - pltpu.roll(dk, HALF, 1) * sine).astype(BF16)
        dv = dv_ref[:, cols] + dot(kr_ref[:, cols], later, ((1,), (0,)))
        gv_ref[:, cols] = (dv * scale).astype(BF16)


def call(kernel, outs, in_specs, cost):
    return pl.pallas_call(
        kernel,
        out_shape=tuple(jax.ShapeDtypeStruct(s, d) for s, d in outs),
        in_specs=in_specs,
        out_specs=tuple(WHOLE for _ in outs),
        compiler_params=params(),
        cost_estimate=pl.CostEstimate(flops=cost[0], bytes_accessed=cost[1], transcendentals=0),
    )


def shards(queries, keys, values, grad_out, positions):
    ny, nz, nx = lax.axis_size("y"), lax.axis_size("z"), lax.axis_size("x")
    scale = 1.0 / math.sqrt(HEAD_DIM * BLOCK * ny * nz * nx * 2)
    core = lax.axis_index("core")
    core_s = core.astype(jnp.int32)[None]
    wide, state = (BLOCK, WIDTH), (WIDTH, HEAD_DIM)
    qr, kr, cosine, sine, mine, other = call(
        rotate_kernel,
        [(wide, BF16), (wide, BF16), ((BLOCK, HEAD_DIM), F32), ((BLOCK, HEAD_DIM), F32), (state, F32), (state, F32)],
        [SCALAR] + [WHOLE] * 6,
        (2 * 8 * 512 * 128 * 128, 4 << 20),
    )(core_s, positions.reshape(BLOCK // HEAD_DIM, HEAD_DIM), jnp.asarray(FREQUENCY), queries, keys, values, grad_out)

    swap = [(0, 1), (1, 0)]
    chips = nz * nx
    piece = (WIDTH // chips, HEAD_DIM)
    pair = mine + lax.ppermute(other, "core", swap)
    pieces = lax.all_to_all(pair.reshape((chips,) + piece), ("z", "x"), 0, 0)
    total, pre = call(
        scan_kernel, [(piece, F32), ((chips,) + piece, F32)], [SCALAR, WHOLE], (0, 1 << 19)
    )(core_s, pieces)
    y = lax.axis_index("y")
    above = jnp.zeros(piece, F32)
    for step in range(1, ny):
        came = lax.ppermute(total, "y", [(i, (i + step) % ny) for i in range(ny)])
        origin = lax.rem(y - step + ny, ny)
        wanted = jnp.where(core == 0, origin < y, origin > y)
        above = above + jnp.where(wanted, came, 0.0)
    dq, dk, dv = call(
        intra_kernel, [(wide, F32)] * 3, [WHOLE] * 4, (2 * 4 * 6 * 512 * 512 * 128, 5 << 20)
    )(qr, kr, values, grad_out)
    chip = lax.all_to_all(pre + above[None], ("z", "x"), 0, 0).reshape(state)
    came = lax.ppermute(chip + mine, "core", swap)

    def final(*refs):
        final_kernel(*refs, scale=scale)

    return call(
        final, [(wide, BF16)] * 3, [SCALAR] + [WHOLE] * 10, (2 * 4 * 3 * 512 * 128 * 128, 7 << 20)
    )(core_s, chip, came, kr, values, grad_out, cosine, sine, dq, dk, dv)


def solution(mesh):
    ny = mesh.shape["grp"]
    nz, nx = 8, 4
    fine = Mesh(mesh.devices.reshape(ny, nz, nx, 2), ("y", "z", "x", "core"))
    every = ("y", "z", "x", "core")
    return jax.shard_map(
        shards,
        mesh=fine,
        in_specs=(P(every, None),) * 4 + (P(every),),
        out_specs=(P(every, None),) * 3,
        check_vma=False,
    )
```

```python
import math

import numpy as np
import jax
import jax.numpy as jnp
from jax import lax
from jax.experimental import pallas as pl
from jax.experimental.pallas import tpu as pltpu
from jax.sharding import Mesh, PartitionSpec as P

HEADS = 4
HEAD_DIM = 128
BLOCK = 512
THETA = 500000.0
WIDTH = HEADS * HEAD_DIM
HALF = HEAD_DIM // 2
F32 = jnp.float32
BF16 = jnp.bfloat16
VMEM_LIMIT = 48 * 1024 * 1024
WHOLE = pl.BlockSpec(memory_space=pltpu.VMEM)
HBM = pl.BlockSpec(memory_space=pltpu.HBM)
SCALAR = pl.BlockSpec(memory_space=pltpu.SMEM)

FREQUENCY = np.tile(
    np.power(THETA, -2.0 * np.arange(HALF) / HEAD_DIM), 2
).astype(np.float32)[None, :]

HALF_PI = (1.5703125, 4.837512969970703125e-4, 7.54978995489188216e-8)


def params():
    return pltpu.CompilerParams(vmem_limit_bytes=VMEM_LIMIT)


def sin_cos(angle):
    turns = jnp.floor(angle * (2.0 / math.pi) + 0.5)
    r = angle - turns * HALF_PI[0]
    r = r - turns * HALF_PI[1]
    r = r - turns * HALF_PI[2]
    r2 = r * r
    s = r + r * r2 * (-1.6666654611e-1 + r2 * (8.3321608736e-3 + r2 * -1.9515295891e-4))
    c = 1.0 + r2 * (-0.5 + r2 * (4.166664568298827e-2 + r2 * (-1.388731625493765e-3 + r2 * 2.443315711809948e-5)))
    quadrant = turns.astype(jnp.int32) & 3
    odd = (quadrant & 1) == 1
    sine = jnp.where(odd, c, s)
    cosine = jnp.where(odd, s, c)
    sine = jnp.where(quadrant >= 2, -sine, sine)
    cosine = jnp.where((quadrant == 1) | (quadrant == 2), -cosine, cosine)
    return sine, cosine


def dot(a, b, dims):
    return lax.dot_general(a, b, (dims, ((), ())), preferred_element_type=F32)


def rotate_kernel(
    core_ref, pos_hbm, freq_hbm, q_hbm, k_hbm, v_hbm, o_hbm,
    qr_ref, kr_ref, v_ref, o_ref, cos_ref, sin_ref, mine_ref, other_ref,
    pos_ref, freq_ref, q_ref, k_ref, small_sems, sems,
):
    core = core_ref[0]
    small = [
        pltpu.make_async_copy(pos_hbm, pos_ref, small_sems.at[0]),
        pltpu.make_async_copy(freq_hbm, freq_ref, small_sems.at[1]),
    ]
    for copy in small:
        copy.start()
    copies = []
    for h in range(HEADS):
        cols = slice(h * HEAD_DIM, (h + 1) * HEAD_DIM)
        pairs = ((k_hbm, k_ref), (v_hbm, v_ref), (q_hbm, q_ref), (o_hbm, o_ref))
        of_head = [
            pltpu.make_async_copy(src.at[:, cols], dst.at[:, cols], sems.at[4 * h + i])
            for i, (src, dst) in enumerate(pairs)
        ]
        for copy in of_head:
            copy.start()
        copies.append(of_head)
    first = lax.broadcasted_iota(jnp.int32, (HEAD_DIM, HEAD_DIM), 1) < HALF
    for copy in small:
        copy.wait()
    for i in range(BLOCK // HEAD_DIM):
        row = jnp.broadcast_to(pos_ref[i : i + 1, :].astype(F32), (HEAD_DIM, HEAD_DIM))
        sine, cosine = sin_cos(row.T * freq_ref[...])
        rows = slice(i * HEAD_DIM, (i + 1) * HEAD_DIM)
        cos_ref[rows, :] = cosine
        sin_ref[rows, :] = jnp.where(first, -sine, sine)
    for h in range(HEADS):
        for copy in copies[h]:
            copy.wait()
        cosine, sine = cos_ref[...], sin_ref[...]
        cols = slice(h * HEAD_DIM, (h + 1) * HEAD_DIM)
        rows = cols
        k = k_ref[:, cols].astype(F32)
        kr = (k * cosine + pltpu.roll(k, HALF, 1) * sine).astype(BF16)
        kr_ref[:, cols] = kr
        key_state = dot(kr, v_ref[:, cols], ((0,), (0,)))
        q = q_ref[:, cols].astype(F32)
        qr = (q * cosine + pltpu.roll(q, HALF, 1) * sine).astype(BF16)
        qr_ref[:, cols] = qr
        query_state = dot(qr, o_ref[:, cols], ((0,), (0,)))
        mine_ref[rows, :] = jnp.where(core == 0, key_state, query_state)
        other_ref[rows, :] = jnp.where(core == 0, query_state, key_state)


def lower_kernel(a_ref, b_ref, c_ref, out_ref):
    triangle_kernel(a_ref, b_ref, c_ref, out_ref, True)


def upper_kernel(a_ref, b_ref, c_ref, out_ref):
    triangle_kernel(a_ref, b_ref, c_ref, out_ref, False)


def triangle_kernel(a_ref, b_ref, c_ref, out_ref, low):
    n = BLOCK // 2
    row = lax.broadcasted_iota(jnp.int32, (n, n), 0)
    col = lax.broadcasted_iota(jnp.int32, (n, n), 1)
    kept = row >= col if low else row <= col
    halves = (slice(0, n), slice(n, BLOCK))
    one, both = halves if low else halves[::-1]
    for h in range(HEADS):
        cols = slice(h * HEAD_DIM, (h + 1) * HEAD_DIM)

        def part(i, j):
            s = dot(a_ref[i, cols], b_ref[j, cols], ((1,), (1,)))
            if i == j:
                s = jnp.where(kept, s, 0.0)
            return dot(s.astype(BF16), c_ref[j, cols], ((1,), (0,)))

        out_ref[one, cols] = part(one, one)
        out_ref[both, cols] = part(both, one) + part(both, both)


def scan_kernel(core_ref, r_ref, total_ref, pre_ref):
    n = r_ref.shape[0]
    total = r_ref[0]
    for i in range(1, n):
        total = total + r_ref[i]
    total_ref[...] = total
    up = core_ref[0] == 0

    @pl.when(up)
    def _():
        acc = jnp.zeros_like(total)
        for i in range(n):
            pre_ref[i] = acc
            acc = acc + r_ref[i]

    @pl.when(jnp.logical_not(up))
    def _():
        acc = jnp.zeros_like(total)
        for i in reversed(range(n)):
            pre_ref[i] = acc
            acc = acc + r_ref[i]


def final_kernel(
    core_ref, chip_ref, recv_ref, kr_ref, v_ref, o_ref, cos_ref, sin_ref, dq_ref, dk_ref, dv_ref,
    gq_hbm, gk_hbm, gv_hbm, gq_ref, gk_ref, gv_ref, sems, *, scale,
):
    core = core_ref[0]
    copies = []

    def leave(src, dst, cols):
        copy = pltpu.make_async_copy(src.at[:, cols], dst.at[:, cols], sems.at[len(copies)])
        copy.start()
        copies.append(copy)

    cosine = cos_ref[...] * scale
    sine = sin_ref[...] * scale
    for h in range(HEADS):
        cols = slice(h * HEAD_DIM, (h + 1) * HEAD_DIM)
        rows = cols
        chip, recv = chip_ref[rows, :], recv_ref[rows, :]
        prior = jnp.where(core == 0, chip, recv).astype(BF16)
        later = jnp.where(core == 0, recv, chip).astype(BF16)
        dq = dq_ref[:, cols] + dot(o_ref[:, cols], prior, ((1,), (1,)))
        gq_ref[:, cols] = (dq * cosine - pltpu.roll(dq, HALF, 1) * sine).astype(BF16)
        leave(gq_ref, gq_hbm, cols)
        dk = dk_ref[:, cols] + dot(v_ref[:, cols], later, ((1,), (1,)))
        gk_ref[:, cols] = (dk * cosine - pltpu.roll(dk, HALF, 1) * sine).astype(BF16)
        leave(gk_ref, gk_hbm, cols)
        dv = dv_ref[:, cols] + dot(kr_ref[:, cols], later, ((1,), (0,)))
        gv_ref[:, cols] = (dv * scale).astype(BF16)
        leave(gv_ref, gv_hbm, cols)
    for copy in copies:
        copy.wait()


def call(kernel, outs, in_specs, cost, out_spec=WHOLE, scratch=()):
    return pl.pallas_call(
        kernel,
        out_shape=tuple(jax.ShapeDtypeStruct(s, d) for s, d in outs),
        in_specs=in_specs,
        out_specs=tuple(out_spec for _ in outs),
        scratch_shapes=scratch,
        compiler_params=params(),
        cost_estimate=pl.CostEstimate(flops=cost[0], bytes_accessed=cost[1], transcendentals=0),
    )


def shards(queries, keys, values, grad_out, positions):
    ny, nz, nx = lax.axis_size("y"), lax.axis_size("z"), lax.axis_size("x")
    scale = 1.0 / math.sqrt(HEAD_DIM * BLOCK * ny * nz * nx * 2)
    core = lax.axis_index("core")
    core_s = core.astype(jnp.int32)[None]
    wide, state, table = (BLOCK, WIDTH), (WIDTH, HEAD_DIM), (BLOCK, HEAD_DIM)
    groups = BLOCK // HEAD_DIM
    qr, kr, v, o, cosine, sine, mine, other = call(
        rotate_kernel,
        [(wide, BF16)] * 4 + [(table, F32)] * 2 + [(state, F32)] * 2,
        [SCALAR] + [HBM] * 6,
        (2 * 8 * 512 * 128 * 128, 4 << 20),
        scratch=[
            pltpu.VMEM((groups, HEAD_DIM), jnp.int32),
            pltpu.VMEM((1, HEAD_DIM), F32),
            pltpu.VMEM(wide, BF16),
            pltpu.VMEM(wide, BF16),
            pltpu.SemaphoreType.DMA((2,)),
            pltpu.SemaphoreType.DMA((4 * HEADS,)),
        ],
    )(core_s, *[
        pltpu.with_memory_space_constraint(a, pltpu.HBM)
        for a in (positions.reshape(groups, HEAD_DIM), jnp.asarray(FREQUENCY), queries, keys, values, grad_out)
    ])

    def triangle(kernel, a, b, c):
        return call(kernel, [(wide, F32)], [WHOLE] * 3, (2 * 4 * 2 * 512 * 512 * 128, 3 << 20))(a, b, c)[0]

    swap = [(0, 1), (1, 0)]
    chips = nz * nx
    piece = (WIDTH // chips, HEAD_DIM)
    came = lax.ppermute(other, "core", swap)
    dv = triangle(upper_kernel, kr, qr, o)
    came, dv = lax.optimization_barrier((came, dv))
    pieces = lax.all_to_all((mine + came).reshape((chips,) + piece), ("z", "x"), 0, 0)
    total, pre = call(
        scan_kernel, [(piece, F32), ((chips,) + piece, F32)], [SCALAR, WHOLE], (0, 1 << 19)
    )(core_s, pieces)
    y = lax.axis_index("y")
    total, o, v = lax.optimization_barrier((total, o, v))
    others = [lax.ppermute(total, "y", [(i, i ^ step) for i in range(ny)]) for step in (2, 3, 1)]
    dq = triangle(lower_kernel, o, v, kr)
    dk = triangle(upper_kernel, v, o, qr)
    others, dq, dk = lax.optimization_barrier((others, dq, dk))
    above = jnp.zeros(piece, F32)
    for step, came in zip((2, 3, 1), others):
        wanted = jnp.where(core == 0, (y ^ step) < y, (y ^ step) > y)
        above = above + jnp.where(wanted, came, 0.0)
    chip = lax.all_to_all(pre + above[None], ("z", "x"), 0, 0).reshape(state)
    came = lax.ppermute(chip + mine, "core", swap)

    def final(*refs):
        final_kernel(*refs, scale=scale)

    return call(
        final,
        [(wide, BF16)] * 3,
        [SCALAR] + [WHOLE] * 10,
        (2 * 4 * 3 * 512 * 128 * 128, 7 << 20),
        out_spec=HBM,
        scratch=[pltpu.VMEM(wide, BF16)] * 3 + [pltpu.SemaphoreType.DMA((3 * HEADS,))],
    )(core_s, chip, came, kr, v, o, cosine, sine, dq, dk, dv)


def solution(mesh):
    ny = mesh.shape["grp"]
    nz, nx = 8, 4
    fine = Mesh(mesh.devices.reshape(ny, nz, nx, 2), ("y", "z", "x", "core"))
    every = ("y", "z", "x", "core")
    return jax.shard_map(
        shards,
        mesh=fine,
        in_specs=(P(every, None),) * 4 + (P(every),),
        out_specs=(P(every, None),) * 3,
        check_vma=False,
    )
```

```python
import math

import numpy as np
import jax
import jax.numpy as jnp
from jax import lax
from jax.experimental import pallas as pl
from jax.experimental.pallas import tpu as pltpu
from jax.sharding import Mesh, PartitionSpec as P

HEADS = 4
HEAD_DIM = 128
BLOCK = 512
THETA = 500000.0
WIDTH = HEADS * HEAD_DIM
HALF = HEAD_DIM // 2
F32 = jnp.float32
BF16 = jnp.bfloat16
VMEM_LIMIT = 16 * 1024 * 1024
WHOLE = pl.BlockSpec(memory_space=pltpu.VMEM)
HBM = pl.BlockSpec(memory_space=pltpu.HBM)
SCALAR = pl.BlockSpec(memory_space=pltpu.SMEM)

FREQUENCY = np.tile(
    np.power(THETA, -2.0 * np.arange(HALF) / HEAD_DIM), 2
).astype(np.float32)[None, :]

HALF_PI = (1.5703125, 4.837512969970703125e-4, 7.54978995489188216e-8)


def params():
    return pltpu.CompilerParams(vmem_limit_bytes=VMEM_LIMIT)


def sin_cos(angle):
    turns = jnp.floor(angle * (2.0 / math.pi) + 0.5)
    r = angle - turns * HALF_PI[0]
    r = r - turns * HALF_PI[1]
    r = r - turns * HALF_PI[2]
    r2 = r * r
    s = r + r * r2 * (-1.6666654611e-1 + r2 * (8.3321608736e-3 + r2 * -1.9515295891e-4))
    c = 1.0 + r2 * (-0.5 + r2 * (4.166664568298827e-2 + r2 * (-1.388731625493765e-3 + r2 * 2.443315711809948e-5)))
    quadrant = turns.astype(jnp.int32) & 3
    odd = (quadrant & 1) == 1
    sine = jnp.where(odd, c, s)
    cosine = jnp.where(odd, s, c)
    sine = jnp.where(quadrant >= 2, -sine, sine)
    cosine = jnp.where((quadrant == 1) | (quadrant == 2), -cosine, cosine)
    return sine, cosine


def dot(a, b, dims):
    return lax.dot_general(a, b, (dims, ((), ())), preferred_element_type=F32)


def rotate_kernel(
    where_ref, _, pos_hbm, freq_hbm, q_hbm, k_hbm, v_hbm, o_hbm,
    qr_ref, kr_ref, v_ref, o_ref, cos_ref, sin_ref, mine_ref, other_ref,
    pos_ref, freq_ref, q_ref, k_ref, small_sems, sems,
):
    core = where_ref[0]
    small = [
        pltpu.make_async_copy(pos_hbm, pos_ref, small_sems.at[0]),
        pltpu.make_async_copy(freq_hbm, freq_ref, small_sems.at[1]),
    ]
    for copy in small:
        copy.start()
    copies = []
    for src, dst in ((k_hbm, k_ref), (v_hbm, v_ref), (q_hbm, q_ref), (o_hbm, o_ref)):
        of_array = [
            pltpu.make_async_copy(src.at[rows, :], dst.at[rows, :], sems.at[len(copies) * 1 + i])
            for i, rows in enumerate(slice(r * 512, (r + 1) * 512) for r in range(1))
        ]
        copies.append(of_array)
    for copy in copies[0] + copies[1]:
        copy.start()
    first = lax.broadcasted_iota(jnp.int32, (HEAD_DIM, HEAD_DIM), 1) < HALF
    for copy in small:
        copy.wait()
    for copy in copies[2] + copies[3]:
        copy.start()
    for i in range(BLOCK // HEAD_DIM):
        row = jnp.broadcast_to(pos_ref[i : i + 1, :].astype(F32), (HEAD_DIM, HEAD_DIM))
        sine, cosine = sin_cos(row.T * freq_ref[...])
        rows = slice(i * HEAD_DIM, (i + 1) * HEAD_DIM)
        cos_ref[rows, :] = cosine
        sin_ref[rows, :] = jnp.where(first, -sine, sine)
    def rotated(ref, out_ref, other_ref):
        states = []
        for h in range(HEADS):
            cols = slice(h * HEAD_DIM, (h + 1) * HEAD_DIM)
            a = ref[:, cols].astype(F32)
            rot = (a * cos_ref[...] + pltpu.roll(a, HALF, 1) * sin_ref[...]).astype(BF16)
            out_ref[:, cols] = rot
            states.append(dot(other_ref[:, cols], rot, ((0,), (0,))))
        return states

    for copy in copies[0] + copies[1]:
        copy.wait()
    key_states = rotated(k_ref, kr_ref, v_ref)
    for h in range(HEADS):
        rows = slice(h * HEAD_DIM, (h + 1) * HEAD_DIM)
        mine_ref[rows, :] = key_states[h]
        other_ref[rows, :] = key_states[h]
    for copy in copies[2] + copies[3]:
        copy.wait()
    query_states = rotated(q_ref, qr_ref, o_ref)
    for h in range(HEADS):
        rows = slice(h * HEAD_DIM, (h + 1) * HEAD_DIM)
        mine_ref[rows, :] = jnp.where(core == 0, mine_ref[rows, :], query_states[h])
        other_ref[rows, :] = jnp.where(core == 0, query_states[h], other_ref[rows, :])


def triangle(a_ref, b_ref, c_ref, h, low):
    n = BLOCK // 2
    row = lax.broadcasted_iota(jnp.int32, (n, n), 0)
    col = lax.broadcasted_iota(jnp.int32, (n, n), 1)
    kept = row >= col if low else row <= col
    cols = slice(h * HEAD_DIM, (h + 1) * HEAD_DIM)
    halves = (slice(0, n), slice(n, BLOCK))

    def part(i, j):
        s = dot(a_ref[halves[i], cols], b_ref[halves[j], cols], ((1,), (1,)))
        if i == j:
            s = jnp.where(kept, s, 0.0)
        return dot(s.astype(BF16), c_ref[halves[j], cols], ((1,), (0,)))

    if low:
        return part(0, 0), part(1, 0) + part(1, 1)
    return part(0, 0) + part(0, 1), part(1, 1)


BESIDE_FIRST = (("dv", 0), ("dv", 1), ("dv", 2))
BESIDE_GROUPS = (("dq", 0), ("dq", 1), ("dq", 2), ("dq", 3), ("dk", 0), ("dk", 1))
BESIDE_LAST = (("dk", 2), ("dk", 3), ("dv", 3))
Y_STEPS = (1, 3, 2)


def intra_kernel(qr_ref, kr_ref, v_ref, o_ref, out_ref, *, jobs):
    n = BLOCK // 2
    for i, (kind, h) in enumerate(jobs):
        cols = slice(i * HEAD_DIM, (i + 1) * HEAD_DIM)
        if kind == "dq":
            top, low = triangle(o_ref, v_ref, kr_ref, h, True)
        elif kind == "dk":
            top, low = triangle(v_ref, o_ref, qr_ref, h, False)
        else:
            top, low = triangle(kr_ref, qr_ref, o_ref, h, False)
        out_ref[:n, cols] = top
        out_ref[n:, cols] = low


def scan_kernel(where_ref, r_ref, total_ref, pre_ref):
    n = r_ref.shape[0]
    total = r_ref[0]
    for i in range(1, n):
        total = total + r_ref[i]
    total_ref[...] = total
    up = where_ref[0] == 0

    @pl.when(up)
    def _():
        acc = jnp.zeros_like(total)
        for i in range(n):
            pre_ref[i] = acc
            acc = acc + r_ref[i]

    @pl.when(jnp.logical_not(up))
    def _():
        acc = jnp.zeros_like(total)
        for i in reversed(range(n)):
            pre_ref[i] = acc
            acc = acc + r_ref[i]


def pair_kernel(mine_ref, came_ref, _, out_ref):
    out_ref[...] = mine_ref[...] + came_ref[...]


def place_kernel(where_ref, group_ref, pre_ref, a_ref, b_ref, c_ref, _, out_ref):
    above = jnp.zeros(a_ref.shape, F32)
    up, y = where_ref[0] == 0, group_ref[0]
    for step, ref in zip(Y_STEPS, (a_ref, b_ref, c_ref)):
        below = (y ^ step) < y
        above = above + jnp.where(up == below, ref[...], 0.0)
    out_ref[...] = pre_ref[...] + above[None]


def final_kernel(
    where_ref, chip_ref, recv_ref, kr_ref, v_ref, o_ref, cos_ref, sin_ref, first_ref, groups_ref, last_ref,
    gq_hbm, gk_hbm, gv_hbm, gq_ref, gk_ref, gv_ref, sems, *, scale,
):
    core = where_ref[0]
    copies = []

    def intra(kind, h):
        for ref, jobs in ((first_ref, BESIDE_FIRST), (groups_ref, BESIDE_GROUPS), (last_ref, BESIDE_LAST)):
            if (kind, h) in jobs:
                i = jobs.index((kind, h))
                return ref[:, i * HEAD_DIM : (i + 1) * HEAD_DIM]

    def leave(src, dst, cols):
        copy = pltpu.make_async_copy(src.at[:, cols], dst.at[:, cols], sems.at[len(copies)])
        copy.start()
        copies.append(copy)

    cosine = cos_ref[...] * scale
    sine = sin_ref[...] * scale
    for h in range(HEADS):
        cols = slice(h * HEAD_DIM, (h + 1) * HEAD_DIM)
        rows = cols
        chip, recv = chip_ref[rows, :], recv_ref[rows, :]
        prior = jnp.where(core == 0, chip, recv).astype(BF16)
        later = jnp.where(core == 0, recv, chip).astype(BF16)
        dq = intra("dq", h) + dot(o_ref[:, cols], prior, ((1,), (0,)))
        gq_ref[:, cols] = (dq * cosine - pltpu.roll(dq, HALF, 1) * sine).astype(BF16)
        leave(gq_ref, gq_hbm, cols)
        dk = intra("dk", h) + dot(v_ref[:, cols], later, ((1,), (0,)))
        gk_ref[:, cols] = (dk * cosine - pltpu.roll(dk, HALF, 1) * sine).astype(BF16)
        leave(gk_ref, gk_hbm, cols)
        dv = intra("dv", h) + dot(kr_ref[:, cols], later, ((1,), (1,)))
        gv_ref[:, cols] = (dv * scale).astype(BF16)
        leave(gv_ref, gv_hbm, cols)
    for copy in copies:
        copy.wait()


def call(kernel, outs, in_specs, cost, out_spec=WHOLE, scratch=()):
    return pl.pallas_call(
        kernel,
        out_shape=tuple(jax.ShapeDtypeStruct(s, d) for s, d in outs),
        in_specs=in_specs,
        out_specs=tuple(out_spec for _ in outs),
        scratch_shapes=scratch,
        compiler_params=params(),
        cost_estimate=pl.CostEstimate(flops=cost[0], bytes_accessed=cost[1], transcendentals=0),
    )


def shards(queries, keys, values, grad_out, positions):
    ny, nz, nx = lax.axis_size("y"), lax.axis_size("z"), lax.axis_size("x")
    scale = 1.0 / math.sqrt(HEAD_DIM * BLOCK * ny * nz * nx * 2)
    where = lax.axis_index("core").astype(jnp.int32)[None]
    group = lax.axis_index("y").astype(jnp.int32)[None]
    wide, state, table = (BLOCK, WIDTH), (WIDTH, HEAD_DIM), (BLOCK, HEAD_DIM)
    groups = BLOCK // HEAD_DIM
    qr, kr, v, o, cosine, sine, mine, other = call(
        rotate_kernel,
        [(wide, BF16)] * 4 + [(table, F32)] * 2 + [(state, F32)] * 2,
        [SCALAR] * 2 + [HBM] * 6,
        (2 * 8 * 512 * 128 * 128, 4 << 20),
        scratch=[
            pltpu.VMEM((groups, HEAD_DIM), jnp.int32),
            pltpu.VMEM((1, HEAD_DIM), F32),
            pltpu.VMEM(wide, BF16),
            pltpu.VMEM(wide, BF16),
            pltpu.SemaphoreType.DMA((2,)),
            pltpu.SemaphoreType.DMA((4 * HEADS,)),
        ],
    )(where, group, *[
        pltpu.with_memory_space_constraint(a, pltpu.HBM)
        for a in (positions.reshape(groups, HEAD_DIM), jnp.asarray(FREQUENCY), queries, keys, values, grad_out)
    ])

    def intra(jobs, after=()):
        def kernel(*refs):
            intra_kernel(*refs[:4], refs[-1], jobs=jobs)

        shape = (BLOCK, len(jobs) * HEAD_DIM)
        work = 2 * len(jobs) * 2 * BLOCK * BLOCK * HEAD_DIM
        specs = [WHOLE] * (4 + len(after))
        return call(kernel, [(shape, F32)], specs, (work, 3 << 20))(qr, kr, v, o, *after)[0]

    swap = [(0, 1), (1, 0)]
    chips = nz * nx
    piece = (WIDTH // chips, HEAD_DIM)
    came = lax.ppermute(other, "core", swap)
    first = intra(BESIDE_FIRST)
    (pair,) = call(pair_kernel, [(state, F32)], [WHOLE] * 3, (0, 1 << 19))(mine, came, first)
    pieces = lax.all_to_all(pair.reshape((chips,) + piece), ("z", "x"), 0, 0)
    total, pre = call(
        scan_kernel, [(piece, F32), ((chips,) + piece, F32)], [SCALAR, WHOLE], (0, 1 << 19)
    )(where, pieces)
    groups = intra(BESIDE_GROUPS, (total,))
    others = [lax.ppermute(total, "y", [(i, i ^ step) for i in range(ny)]) for step in Y_STEPS]
    (place,) = call(
        place_kernel, [((chips,) + piece, F32)], [SCALAR] * 2 + [WHOLE] * 5, (0, 1 << 19)
    )(where, group, pre, *others, groups)
    chip = lax.all_to_all(place, ("z", "x"), 0, 0).reshape(state)
    last = intra(BESIDE_LAST, (chip,))
    came = lax.ppermute(chip + mine, "core", swap)

    def final(*refs):
        final_kernel(*refs, scale=scale)

    return call(
        final,
        [(wide, BF16)] * 3,
        [SCALAR] + [WHOLE] * 10,
        (2 * 4 * 3 * 512 * 128 * 128, 7 << 20),
        out_spec=HBM,
        scratch=[pltpu.VMEM(wide, BF16)] * 3 + [pltpu.SemaphoreType.DMA((3 * HEADS,))],
    )(where, chip, came, kr, v, o, cosine, sine, first, groups, last)


def solution(mesh):
    ny = mesh.shape["grp"]
    nz, nx = 8, 4
    fine = Mesh(mesh.devices.reshape(ny, nz, nx, 2), ("y", "z", "x", "core"))
    every = ("y", "z", "x", "core")
    return jax.shard_map(
        shards,
        mesh=fine,
        in_specs=(P(every, None),) * 4 + (P(every),),
        out_specs=(P(every, None),) * 3,
        check_vma=False,
    )
```

```python
import math

import numpy as np
import jax
import jax.numpy as jnp
from jax import lax
from jax.experimental import pallas as pl
from jax.experimental.pallas import tpu as pltpu
from jax.sharding import PartitionSpec as P

HEADS = 4
HEAD_DIM = 128
BLOCK = 512
THETA = 500000.0
WIDTH = HEADS * HEAD_DIM
HALF = HEAD_DIM // 2
F32 = jnp.float32
BF16 = jnp.bfloat16
VMEM_LIMIT = 16 * 1024 * 1024
WHOLE = pl.BlockSpec(memory_space=pltpu.VMEM)
HBM = pl.BlockSpec(memory_space=pltpu.HBM)

FREQUENCY = np.tile(
    np.power(THETA, -2.0 * np.arange(HALF) / HEAD_DIM), 2
).astype(np.float32)[None, :]

HALF_PI = (1.5703125, 4.837512969970703125e-4, 7.54978995489188216e-8)


def params():
    return pltpu.CompilerParams(vmem_limit_bytes=VMEM_LIMIT)


def sin_cos(angle):
    turns = jnp.floor(angle * (2.0 / math.pi) + 0.5)
    r = angle - turns * HALF_PI[0]
    r = r - turns * HALF_PI[1]
    r = r - turns * HALF_PI[2]
    r2 = r * r
    s = r + r * r2 * (-1.6666654611e-1 + r2 * (8.3321608736e-3 + r2 * -1.9515295891e-4))
    c = 1.0 + r2 * (-0.5 + r2 * (4.166664568298827e-2 + r2 * (-1.388731625493765e-3 + r2 * 2.443315711809948e-5)))
    quadrant = turns.astype(jnp.int32) & 3
    odd = (quadrant & 1) == 1
    sine = jnp.where(odd, c, s)
    cosine = jnp.where(odd, s, c)
    sine = jnp.where(quadrant >= 2, -sine, sine)
    cosine = jnp.where((quadrant == 1) | (quadrant == 2), -cosine, cosine)
    return sine, cosine


def dot(a, b, dims):
    return lax.dot_general(a, b, (dims, ((), ())), preferred_element_type=F32)


def rotate_kernel(
    pos_hbm, freq_hbm, q_hbm, k_hbm, v_hbm, o_hbm,
    qr_ref, kr_ref, v_ref, o_ref, cos_ref, sin_ref, mine_ref, other_ref,
    pos_ref, freq_ref, q_ref, k_ref, small_sems, sems,
):
    core = (lax.axis_index("stretch") & 1)
    small = [
        pltpu.make_async_copy(pos_hbm, pos_ref, small_sems.at[0]),
        pltpu.make_async_copy(freq_hbm, freq_ref, small_sems.at[1]),
    ]
    for copy in small:
        copy.start()
    pairs = ((k_hbm, k_ref), (v_hbm, v_ref), (q_hbm, q_ref), (o_hbm, o_ref))
    copies = [pltpu.make_async_copy(src, dst, sems.at[i]) for i, (src, dst) in enumerate(pairs)]
    for copy in copies[:2]:
        copy.start()
    first = lax.broadcasted_iota(jnp.int32, (HEAD_DIM, HEAD_DIM), 1) < HALF
    for copy in small:
        copy.wait()
    for copy in copies[2:]:
        copy.start()
    for i in range(BLOCK // HEAD_DIM):
        row = jnp.broadcast_to(pos_ref[i : i + 1, :].astype(F32), (HEAD_DIM, HEAD_DIM))
        sine, cosine = sin_cos(row.T * freq_ref[...])
        rows = slice(i * HEAD_DIM, (i + 1) * HEAD_DIM)
        cos_ref[rows, :] = cosine
        sin_ref[rows, :] = jnp.where(first, -sine, sine)

    def rotated(ref, out_ref, other_ref):
        states = []
        for h in range(HEADS):
            cols = slice(h * HEAD_DIM, (h + 1) * HEAD_DIM)
            a = ref[:, cols].astype(F32)
            rot = (a * cos_ref[...] + pltpu.roll(a, HALF, 1) * sin_ref[...]).astype(BF16)
            out_ref[:, cols] = rot
            states.append(dot(other_ref[:, cols], rot, ((0,), (0,))))
        return states

    for copy in copies[:2]:
        copy.wait()
    key_states = rotated(k_ref, kr_ref, v_ref)
    for h in range(HEADS):
        rows = slice(h * HEAD_DIM, (h + 1) * HEAD_DIM)
        mine_ref[rows, :] = key_states[h]
        other_ref[rows, :] = key_states[h]
    for copy in copies[2:]:
        copy.wait()
    query_states = rotated(q_ref, qr_ref, o_ref)
    for h in range(HEADS):
        rows = slice(h * HEAD_DIM, (h + 1) * HEAD_DIM)
        mine_ref[rows, :] = jnp.where(core == 0, mine_ref[rows, :], query_states[h])
        other_ref[rows, :] = jnp.where(core == 0, query_states[h], other_ref[rows, :])


def triangle(a_ref, b_ref, c_ref, h, low):
    n = BLOCK // 2
    row = lax.broadcasted_iota(jnp.int32, (n, n), 0)
    col = lax.broadcasted_iota(jnp.int32, (n, n), 1)
    kept = row >= col if low else row <= col
    cols = slice(h * HEAD_DIM, (h + 1) * HEAD_DIM)
    halves = (slice(0, n), slice(n, BLOCK))

    def part(i, j):
        s = dot(a_ref[halves[i], cols], b_ref[halves[j], cols], ((1,), (1,)))
        if i == j:
            s = jnp.where(kept, s, 0.0)
        return dot(s.astype(BF16), c_ref[halves[j], cols], ((1,), (0,)))

    if low:
        return part(0, 0), part(1, 0) + part(1, 1)
    return part(0, 0) + part(0, 1), part(1, 1)


BESIDE_FIRST = (("dv", 0), ("dv", 1), ("dv", 2))
BESIDE_GROUPS = tuple(("dq", h) for h in range(HEADS)) + tuple(("dk", h) for h in range(HEADS)) + (("dv", 3),)
Y_STEPS = (1, 3, 2)


def intra_kernel(qr_ref, kr_ref, v_ref, o_ref, out_ref, *, jobs):
    n = BLOCK // 2
    for i, (kind, h) in enumerate(jobs):
        cols = slice(i * HEAD_DIM, (i + 1) * HEAD_DIM)
        if kind == "dq":
            top, low = triangle(o_ref, v_ref, kr_ref, h, True)
        elif kind == "dk":
            top, low = triangle(v_ref, o_ref, qr_ref, h, False)
        else:
            top, low = triangle(kr_ref, qr_ref, o_ref, h, False)
        out_ref[:n, cols] = top
        out_ref[n:, cols] = low


def scan_kernel(r_ref, total_ref, pre_ref):
    n = r_ref.shape[0]
    token_order = sorted(range(n), key=lambda i: ORDER[i])
    total = r_ref[0]
    for i in range(1, n):
        total = total + r_ref[i]
    total_ref[...] = total
    up = (lax.axis_index("stretch") & 1) == 0

    @pl.when(up)
    def _():
        acc = jnp.zeros_like(total)
        for i in token_order:
            pre_ref[i] = acc
            acc = acc + r_ref[i]

    @pl.when(jnp.logical_not(up))
    def _():
        acc = jnp.zeros_like(total)
        for i in reversed(token_order):
            pre_ref[i] = acc
            acc = acc + r_ref[i]


def pair_kernel(mine_ref, came_ref, _, out_ref):
    out_ref[...] = mine_ref[...] + came_ref[...]


def place_kernel(pre_ref, a_ref, b_ref, c_ref, _, out_ref):
    above = jnp.zeros(a_ref.shape, F32)
    up, y = (lax.axis_index("stretch") & 1) == 0, lax.axis_index("grp")
    for step, ref in zip(Y_STEPS, (a_ref, b_ref, c_ref)):
        below = (y ^ step) < y
        above = above + jnp.where(up == below, ref[...], 0.0)
    out_ref[...] = pre_ref[...] + above[None]


def write_gradients(kinds, prior, later, refs, *, scale):
    kr_ref, v_ref, o_ref, cos_ref, sin_ref, first_ref, groups_ref, outs, held, sems = refs
    copies = []

    def intra(kind, h):
        for ref, jobs in ((first_ref, BESIDE_FIRST), (groups_ref, BESIDE_GROUPS)):
            if (kind, h) in jobs:
                i = jobs.index((kind, h))
                return ref[:, i * HEAD_DIM : (i + 1) * HEAD_DIM]

    cosine = cos_ref[...] * scale
    sine = sin_ref[...] * scale
    for h in range(HEADS):
        cols = slice(h * HEAD_DIM, (h + 1) * HEAD_DIM)
        for kind in kinds:
            if kind == "dv":
                state = later[cols, :].astype(BF16)
                grad = (intra(kind, h) + dot(kr_ref[:, cols], state, ((1,), (1,)))) * scale
            else:
                rows_ref, state = (o_ref, prior) if kind == "dq" else (v_ref, later)
                grad = intra(kind, h) + dot(rows_ref[:, cols], state[cols, :].astype(BF16), ((1,), (0,)))
                grad = grad * cosine - pltpu.roll(grad, HALF, 1) * sine
            place = KINDS.index(kind)
            held[place][:, cols] = grad.astype(BF16)
            copy = pltpu.make_async_copy(held[place].at[:, cols], outs[place].at[:, cols], sems.at[len(copies)])
            copy.start()
            copies.append(copy)
    for copy in copies:
        copy.wait()


ORDER = [z * 4 + x for z in (4, 5, 6, 7, 0, 1, 2, 3) for x in (2, 3, 0, 1)]
GROUPS = [[2 * p + c for p in ORDER] for c in range(2)]

KINDS = ("dq", "dk", "dv")


def own_kernel(chip_ref, *refs, scale):
    refs = (*refs[:7], refs[7:10], refs[10:13], refs[13])
    core = (lax.axis_index("stretch") & 1)

    @pl.when(core == 0)
    def _():
        write_gradients(("dq",), chip_ref, None, refs, scale=scale)

    @pl.when(core != 0)
    def _():
        write_gradients(("dk", "dv"), None, chip_ref, refs, scale=scale)


def final_kernel(came_ref, *refs, scale):
    refs = (*refs[:7], refs[10:13], refs[13:16], refs[16])
    core = (lax.axis_index("stretch") & 1)

    @pl.when(core == 0)
    def _():
        write_gradients(("dk", "dv"), None, came_ref, refs, scale=scale)

    @pl.when(core != 0)
    def _():
        write_gradients(("dq",), came_ref, None, refs, scale=scale)


def call(kernel, outs, in_specs, cost, out_spec=WHOLE, scratch=(), aliases=None):
    return pl.pallas_call(
        kernel,
        out_shape=tuple(jax.ShapeDtypeStruct(s, d) for s, d in outs),
        in_specs=in_specs,
        out_specs=tuple(out_spec for _ in outs),
        scratch_shapes=scratch,
        input_output_aliases=aliases or {},
        compiler_params=params(),
        cost_estimate=pl.CostEstimate(flops=cost[0], bytes_accessed=cost[1], transcendentals=0),
    )


def shards(queries, keys, values, grad_out, positions):
    ny = lax.axis_size("grp")
    scale = 1.0 / math.sqrt(HEAD_DIM * BLOCK * ny * lax.axis_size("stretch"))
    wide, state, table = (BLOCK, WIDTH), (WIDTH, HEAD_DIM), (BLOCK, HEAD_DIM)
    groups = BLOCK // HEAD_DIM
    qr, kr, v, o, cosine, sine, mine, other = call(
        rotate_kernel,
        [(wide, BF16)] * 4 + [(table, F32)] * 2 + [(state, F32)] * 2,
        [HBM] * 6,
        (2 * 8 * 512 * 128 * 128, 4 << 20),
        scratch=[
            pltpu.VMEM((groups, HEAD_DIM), jnp.int32),
            pltpu.VMEM((1, HEAD_DIM), F32),
            pltpu.VMEM(wide, BF16),
            pltpu.VMEM(wide, BF16),
            pltpu.SemaphoreType.DMA((2,)),
            pltpu.SemaphoreType.DMA((4,)),
        ],
    )(*[
        pltpu.with_memory_space_constraint(a, pltpu.HBM)
        for a in (positions.reshape(groups, HEAD_DIM), jnp.asarray(FREQUENCY), queries, keys, values, grad_out)
    ])

    def intra(jobs, after=()):
        def kernel(*refs):
            intra_kernel(*refs[:4], refs[-1], jobs=jobs)

        shape = (BLOCK, len(jobs) * HEAD_DIM)
        work = 2 * len(jobs) * 2 * BLOCK * BLOCK * HEAD_DIM
        specs = [WHOLE] * (4 + len(after))
        return call(kernel, [(shape, F32)], specs, (work, 3 << 20))(qr, kr, v, o, *after)[0]

    swap = [(i, i ^ 1) for i in range(2 * len(ORDER))]
    chips = len(ORDER)
    piece = (WIDTH // chips, HEAD_DIM)
    came = lax.ppermute(other, "stretch", swap)
    first = intra(BESIDE_FIRST)
    (pair,) = call(pair_kernel, [(state, F32)], [WHOLE] * 3, (0, 1 << 19))(mine, came, first)
    pieces = lax.all_to_all(pair.reshape((chips,) + piece), "stretch", 0, 0, axis_index_groups=GROUPS)
    total, pre = call(
        scan_kernel, [(piece, F32), ((chips,) + piece, F32)], [WHOLE], (0, 1 << 19)
    )(pieces)
    groups = intra(BESIDE_GROUPS, (total,))
    others = [lax.ppermute(total, "grp", [(i, i ^ step) for i in range(ny)]) for step in Y_STEPS]
    (place,) = call(
        place_kernel, [((chips,) + piece, F32)], [WHOLE] * 5, (0, 1 << 19)
    )(pre, *others, groups)
    chip = lax.all_to_all(place, "stretch", 0, 0, axis_index_groups=GROUPS).reshape(state)
    came = lax.ppermute(chip + mine, "stretch", swap)

    def own(*refs):
        own_kernel(*refs, scale=scale)

    def final(*refs):
        final_kernel(*refs, scale=scale)

    held = [pltpu.VMEM(wide, BF16)] * 3 + [pltpu.SemaphoreType.DMA((2 * HEADS,))]
    common = (kr, v, o, cosine, sine, first, groups)
    work = (2 * 4 * 2 * 512 * 128 * 128, 4 << 20)
    begun = call(own, [(wide, BF16)] * 3, [WHOLE] * 8, work, out_spec=HBM, scratch=held)(chip, *common)
    return call(
        final, [(wide, BF16)] * 3, [WHOLE] * 8 + [HBM] * 3, work, out_spec=HBM, scratch=held,
        aliases={8: 0, 9: 1, 10: 2},
    )(came, *common, *begun)


def solution(mesh):
    every = ("grp", "stretch")
    return jax.shard_map(
        shards,
        mesh=mesh,
        in_specs=(P(every, None),) * 4 + (P(every),),
        out_specs=(P(every, None),) * 3,
        check_vma=False,
    )
```

```python
import math

import numpy as np
import jax
import jax.numpy as jnp
from jax import lax
from jax.experimental import pallas as pl
from jax.experimental.pallas import tpu as pltpu
from jax.sharding import PartitionSpec as P

HEADS = 4
HEAD_DIM = 128
BLOCK = 512
THETA = 500000.0
WIDTH = HEADS * HEAD_DIM
HALF = HEAD_DIM // 2
F32 = jnp.float32
BF16 = jnp.bfloat16
VMEM_LIMIT = 16 * 1024 * 1024
WHOLE = pl.BlockSpec(memory_space=pltpu.VMEM)
HBM = pl.BlockSpec(memory_space=pltpu.HBM)

FREQUENCY = np.tile(
    np.power(THETA, -2.0 * np.arange(HALF) / HEAD_DIM), 2
).astype(np.float32)[None, :]

HALF_PI = (1.5703125, 4.837512969970703125e-4, 7.54978995489188216e-8)


def params():
    return pltpu.CompilerParams(vmem_limit_bytes=VMEM_LIMIT)


def sin_cos(angle):
    turns = jnp.floor(angle * (2.0 / math.pi) + 0.5)
    r = angle - turns * HALF_PI[0]
    r = r - turns * HALF_PI[1]
    r = r - turns * HALF_PI[2]
    r2 = r * r
    s = r + r * r2 * (-1.6666654611e-1 + r2 * (8.3321608736e-3 + r2 * -1.9515295891e-4))
    c = 1.0 + r2 * (-0.5 + r2 * (4.166664568298827e-2 + r2 * (-1.388731625493765e-3 + r2 * 2.443315711809948e-5)))
    quadrant = turns.astype(jnp.int32) & 3
    odd = (quadrant & 1) == 1
    sine = jnp.where(odd, c, s)
    cosine = jnp.where(odd, s, c)
    sine = jnp.where(quadrant >= 2, -sine, sine)
    cosine = jnp.where((quadrant == 1) | (quadrant == 2), -cosine, cosine)
    return sine, cosine


def dot(a, b, dims):
    return lax.dot_general(a, b, (dims, ((), ())), preferred_element_type=F32)


def rotate_kernel(
    pos_hbm, freq_hbm, q_hbm, k_hbm, v_hbm, o_hbm,
    qr_ref, kr_ref, v_ref, o_ref, cos_ref, sin_ref, mine_ref, other_ref,
    pos_ref, freq_ref, q_ref, k_ref, small_sems, sems,
):
    keys_here = on_keys()
    small = [
        pltpu.make_async_copy(pos_hbm, pos_ref, small_sems.at[0]),
        pltpu.make_async_copy(freq_hbm, freq_ref, small_sems.at[1]),
    ]
    for copy in small:
        copy.start()
    pairs = ((k_hbm, k_ref), (v_hbm, v_ref), (q_hbm, q_ref), (o_hbm, o_ref))
    copies = [pltpu.make_async_copy(src, dst, sems.at[i]) for i, (src, dst) in enumerate(pairs)]
    for copy in copies[:2]:
        copy.start()
    first = lax.broadcasted_iota(jnp.int32, (HEAD_DIM, HEAD_DIM), 1) < HALF
    for copy in small:
        copy.wait()
    for copy in copies[2:]:
        copy.start()
    for i in range(BLOCK // HEAD_DIM):
        row = jnp.broadcast_to(pos_ref[i : i + 1, :].astype(F32), (HEAD_DIM, HEAD_DIM))
        sine, cosine = sin_cos(row.T * freq_ref[...])
        rows = slice(i * HEAD_DIM, (i + 1) * HEAD_DIM)
        cos_ref[rows, :] = cosine
        sin_ref[rows, :] = jnp.where(first, -sine, sine)

    def rotated(ref, out_ref, other_ref):
        states = []
        for h in range(HEADS):
            cols = slice(h * HEAD_DIM, (h + 1) * HEAD_DIM)
            a = ref[:, cols].astype(F32)
            rot = (a * cos_ref[...] + pltpu.roll(a, HALF, 1) * sin_ref[...]).astype(BF16)
            out_ref[:, cols] = rot
            states.append(dot(other_ref[:, cols], rot, ((0,), (0,))))
        return states

    for copy in copies[:2]:
        copy.wait()
    key_states = rotated(k_ref, kr_ref, v_ref)
    for h in range(HEADS):
        rows = slice(h * HEAD_DIM, (h + 1) * HEAD_DIM)
        mine_ref[rows, :] = key_states[h]
        other_ref[rows, :] = key_states[h]
    for copy in copies[2:]:
        copy.wait()
    query_states = rotated(q_ref, qr_ref, o_ref)
    for h in range(HEADS):
        rows = slice(h * HEAD_DIM, (h + 1) * HEAD_DIM)
        mine_ref[rows, :] = jnp.where(keys_here, mine_ref[rows, :], query_states[h])
        other_ref[rows, :] = jnp.where(keys_here, query_states[h], other_ref[rows, :])


FLIPPED = (18,)
ORDER = (
    [(18 + i) % 32 for i in range(32)],
    [(22 + i) % 32 for i in range(32)],
)
GROUPS = [[2 * p + (side ^ (p in FLIPPED)) for p in ORDER[side]] for side in range(2)]


def flipped():
    chip = lax.axis_index("stretch") // 2
    found = chip == FLIPPED[0]
    for p in FLIPPED[1:]:
        found = jnp.logical_or(found, chip == p)
    return found


def on_keys():
    return ((lax.axis_index("stretch") & 1) == 0) != flipped()


def triangle(a_ref, b_ref, c_ref, h, low):
    n = BLOCK // 2
    row = lax.broadcasted_iota(jnp.int32, (n, n), 0)
    col = lax.broadcasted_iota(jnp.int32, (n, n), 1)
    kept = row >= col if low else row <= col
    cols = slice(h * HEAD_DIM, (h + 1) * HEAD_DIM)
    halves = (slice(0, n), slice(n, BLOCK))

    def part(i, j):
        s = dot(a_ref[halves[i], cols], b_ref[halves[j], cols], ((1,), (1,)))
        if i == j:
            s = jnp.where(kept, s, 0.0)
        return dot(s.astype(BF16), c_ref[halves[j], cols], ((1,), (0,)))

    if low:
        return part(0, 0), part(1, 0) + part(1, 1)
    return part(0, 0) + part(0, 1), part(1, 1)


BESIDE_FIRST = (("dv", 0), ("dv", 1), ("dv", 2))
BESIDE_GROUPS = tuple(("dq", h) for h in range(HEADS)) + (("dv", 3),)
EXTRA = tuple(("dk", h) for h in range(HEADS))
Y_STEPS = (1, 3, 2)


def run_jobs(jobs, refs, out_ref):
    qr_ref, kr_ref, v_ref, o_ref = refs
    n = BLOCK // 2
    for i, (kind, h) in enumerate(jobs):
        cols = slice(i * HEAD_DIM, (i + 1) * HEAD_DIM)
        if kind == "dq":
            top, low = triangle(o_ref, v_ref, kr_ref, h, True)
        elif kind == "dk":
            top, low = triangle(v_ref, o_ref, qr_ref, h, False)
        else:
            top, low = triangle(kr_ref, qr_ref, o_ref, h, False)
        out_ref[:n, cols] = top
        out_ref[n:, cols] = low


def early():
    return lax.axis_index("stretch") < len(ORDER[0]) // 2


def first_kernel(*refs):
    run_jobs(BESIDE_FIRST, refs[:4], refs[4])

    @pl.when(early())
    def _():
        run_jobs(EXTRA, refs[:4], refs[5])


def groups_kernel(*refs):
    run_jobs(BESIDE_GROUPS, refs[:4], refs[5])


def last_kernel(*refs):
    @pl.when(jnp.logical_not(early()))
    def _():
        run_jobs(EXTRA, refs[:4], refs[6])


def scan_kernel(r_ref, total_ref, pre_ref):
    n = r_ref.shape[0]
    before, after = (sorted(range(n), key=lambda i: order[i]) for order in ORDER)
    total = r_ref[0]
    for i in range(1, n):
        total = total + r_ref[i]
    total_ref[...] = total
    up = on_keys()

    @pl.when(up)
    def _():
        acc = jnp.zeros_like(total)
        for i in before:
            pre_ref[i] = acc
            acc = acc + r_ref[i]

    @pl.when(jnp.logical_not(up))
    def _():
        acc = jnp.zeros_like(total)
        for i in reversed(after):
            pre_ref[i] = acc
            acc = acc + r_ref[i]


def pair_kernel(mine_ref, came_ref, _, out_ref):
    out_ref[...] = mine_ref[...] + came_ref[...]


def own_state_kernel(chip_ref, mine_ref, came_ref, own_ref, sent_ref):
    turned = flipped()
    own_ref[...] = chip_ref[...] + jnp.where(turned, came_ref[...], 0.0)
    sent_ref[...] = chip_ref[...] + jnp.where(turned, 0.0, mine_ref[...])


def place_kernel(pre_ref, a_ref, b_ref, c_ref, _, out_ref):
    above = jnp.zeros(a_ref.shape, F32)
    up, y = on_keys(), lax.axis_index("grp")
    for step, ref in zip(Y_STEPS, (a_ref, b_ref, c_ref)):
        below = (y ^ step) < y
        above = above + jnp.where(up == below, ref[...], 0.0)
    out_ref[...] = pre_ref[...] + above[None]


def write_gradients(kinds, prior, later, refs, *, scale):
    kr_ref, v_ref, o_ref, cos_ref, sin_ref, first_ref, groups_ref, extra_ref, outs, held, sems = refs
    copies = []

    def intra(kind, h):
        for ref, jobs in ((first_ref, BESIDE_FIRST), (groups_ref, BESIDE_GROUPS), (extra_ref, EXTRA)):
            if (kind, h) in jobs:
                i = jobs.index((kind, h))
                return ref[:, i * HEAD_DIM : (i + 1) * HEAD_DIM]

    cosine = cos_ref[...] * scale
    sine = sin_ref[...] * scale
    for h in range(HEADS):
        cols = slice(h * HEAD_DIM, (h + 1) * HEAD_DIM)
        for kind in kinds:
            if kind == "dv":
                state = later[cols, :].astype(BF16)
                grad = (intra(kind, h) + dot(kr_ref[:, cols], state, ((1,), (1,)))) * scale
            else:
                rows_ref, state = (o_ref, prior) if kind == "dq" else (v_ref, later)
                grad = intra(kind, h) + dot(rows_ref[:, cols], state[cols, :].astype(BF16), ((1,), (0,)))
                grad = grad * cosine - pltpu.roll(grad, HALF, 1) * sine
            place = KINDS.index(kind)
            held[place][:, cols] = grad.astype(BF16)
            copy = pltpu.make_async_copy(held[place].at[:, cols], outs[place].at[:, cols], sems.at[len(copies)])
            copy.start()
            copies.append(copy)
    for copy in copies:
        copy.wait()


KINDS = ("dq", "dk", "dv")


def own_kernel(chip_ref, *refs, scale):
    refs = (*refs[:8], refs[8:11], refs[11:14], refs[14])
    keys_here = on_keys()

    @pl.when(keys_here)
    def _():
        write_gradients(("dq",), chip_ref, None, refs, scale=scale)

    @pl.when(jnp.logical_not(keys_here))
    def _():
        write_gradients(("dk", "dv"), None, chip_ref, refs, scale=scale)


def final_kernel(came_ref, *refs, scale):
    refs = (*refs[:8], refs[11:14], refs[14:17], refs[17])
    keys_here = on_keys()

    @pl.when(keys_here)
    def _():
        write_gradients(("dk", "dv"), None, came_ref, refs, scale=scale)

    @pl.when(jnp.logical_not(keys_here))
    def _():
        write_gradients(("dq",), came_ref, None, refs, scale=scale)


def call(kernel, outs, in_specs, cost, out_spec=WHOLE, scratch=(), aliases=None):
    return pl.pallas_call(
        kernel,
        out_shape=tuple(jax.ShapeDtypeStruct(s, d) for s, d in outs),
        in_specs=in_specs,
        out_specs=tuple(out_spec for _ in outs),
        scratch_shapes=scratch,
        input_output_aliases=aliases or {},
        compiler_params=params(),
        cost_estimate=pl.CostEstimate(flops=cost[0], bytes_accessed=cost[1], transcendentals=0),
    )


def shards(queries, keys, values, grad_out, positions):
    ny = lax.axis_size("grp")
    scale = 1.0 / math.sqrt(HEAD_DIM * BLOCK * ny * lax.axis_size("stretch"))
    wide, state, table = (BLOCK, WIDTH), (WIDTH, HEAD_DIM), (BLOCK, HEAD_DIM)
    groups = BLOCK // HEAD_DIM
    qr, kr, v, o, cosine, sine, mine, other = call(
        rotate_kernel,
        [(wide, BF16)] * 4 + [(table, F32)] * 2 + [(state, F32)] * 2,
        [HBM] * 6,
        (2 * 8 * 512 * 128 * 128, 4 << 20),
        scratch=[
            pltpu.VMEM((groups, HEAD_DIM), jnp.int32),
            pltpu.VMEM((1, HEAD_DIM), F32),
            pltpu.VMEM(wide, BF16),
            pltpu.VMEM(wide, BF16),
            pltpu.SemaphoreType.DMA((2,)),
            pltpu.SemaphoreType.DMA((4,)),
        ],
    )(*[
        pltpu.with_memory_space_constraint(a, pltpu.HBM)
        for a in (positions.reshape(groups, HEAD_DIM), jnp.asarray(FREQUENCY), queries, keys, values, grad_out)
    ])

    def work(*jobs):
        return (2 * sum(map(len, jobs)) * 2 * BLOCK * BLOCK * HEAD_DIM, 3 << 20)

    def products(*jobs):
        return [((BLOCK, len(each) * HEAD_DIM), F32) for each in jobs]

    swap = [(i, i ^ 1) for i in range(2 * len(ORDER[0]))]
    chips = len(ORDER[0])
    piece = (WIDTH // chips, HEAD_DIM)
    came = lax.ppermute(other, "stretch", swap)
    rows = (qr, kr, v, o)
    first, extra = call(
        first_kernel, products(BESIDE_FIRST, EXTRA), [WHOLE] * 4, work(BESIDE_FIRST)
    )(*rows)
    (pair,) = call(pair_kernel, [(state, F32)], [WHOLE] * 3, (0, 1 << 19))(mine, came, first)
    pieces = lax.all_to_all(pair.reshape((chips,) + piece), "stretch", 0, 0, axis_index_groups=GROUPS)
    total, pre = call(
        scan_kernel, [(piece, F32), ((chips,) + piece, F32)], [WHOLE], (0, 1 << 19)
    )(pieces)
    (groups,) = call(
        groups_kernel, products(BESIDE_GROUPS), [WHOLE] * 5, work(BESIDE_GROUPS)
    )(*rows, total)
    others = [lax.ppermute(total, "grp", [(i, i ^ step) for i in range(ny)]) for step in Y_STEPS]
    (place,) = call(
        place_kernel, [((chips,) + piece, F32)], [WHOLE] * 5, (0, 1 << 19)
    )(pre, *others, groups)
    chip = lax.all_to_all(place, "stretch", 0, 0, axis_index_groups=GROUPS).reshape(state)
    own_state, sent = call(own_state_kernel, [(state, F32)] * 2, [WHOLE] * 3, (0, 1 << 19))(chip, mine, came)
    came = lax.ppermute(sent, "stretch", swap)
    (extra,) = call(
        last_kernel, products(EXTRA), [WHOLE] * 6, work(EXTRA), aliases={5: 0}
    )(*rows, chip, extra)

    def own(*refs):
        own_kernel(*refs, scale=scale)

    def final(*refs):
        final_kernel(*refs, scale=scale)

    held = [pltpu.VMEM(wide, BF16)] * 3 + [pltpu.SemaphoreType.DMA((2 * HEADS,))]
    common = (kr, v, o, cosine, sine, first, groups, extra)
    cost = (2 * 4 * 2 * 512 * 128 * 128, 4 << 20)
    begun = call(own, [(wide, BF16)] * 3, [WHOLE] * 9, cost, out_spec=HBM, scratch=held)(own_state, *common)
    return call(
        final, [(wide, BF16)] * 3, [WHOLE] * 9 + [HBM] * 3, cost, out_spec=HBM, scratch=held,
        aliases={9: 0, 10: 1, 11: 2},
    )(came, *common, *begun)


def solution(mesh):
    every = ("grp", "stretch")
    return jax.shard_map(
        shards,
        mesh=mesh,
        in_specs=(P(every, None),) * 4 + (P(every),),
        out_specs=(P(every, None),) * 3,
        check_vma=False,
    )
```

```python
import math

import numpy as np
import jax
import jax.numpy as jnp
from jax import lax
from jax.experimental import pallas as pl
from jax.experimental.pallas import tpu as pltpu
from jax.sharding import PartitionSpec as P

HEADS = 4
HEAD_DIM = 128
BLOCK = 512
THETA = 500000.0
WIDTH = HEADS * HEAD_DIM
HALF = HEAD_DIM // 2
F32 = jnp.float32
BF16 = jnp.bfloat16
VMEM_LIMIT = 16 * 1024 * 1024
WHOLE = pl.BlockSpec(memory_space=pltpu.VMEM)
HBM = pl.BlockSpec(memory_space=pltpu.HBM)

FREQUENCY = np.tile(
    np.power(THETA, -2.0 * np.arange(HALF) / HEAD_DIM), 2
).astype(np.float32)[None, :]

HALF_PI = (1.5703125, 4.837512969970703125e-4, 7.54978995489188216e-8)


def params():
    return pltpu.CompilerParams(vmem_limit_bytes=VMEM_LIMIT)


def sin_cos(angle):
    turns = jnp.floor(angle * (2.0 / math.pi) + 0.5)
    r = angle - turns * HALF_PI[0]
    r = r - turns * HALF_PI[1]
    r = r - turns * HALF_PI[2]
    r2 = r * r
    s = r + r * r2 * (-1.6666654611e-1 + r2 * (8.3321608736e-3 + r2 * -1.9515295891e-4))
    c = 1.0 + r2 * (-0.5 + r2 * (4.166664568298827e-2 + r2 * (-1.388731625493765e-3 + r2 * 2.443315711809948e-5)))
    quadrant = turns.astype(jnp.int32) & 3
    odd = (quadrant & 1) == 1
    sine = jnp.where(odd, c, s)
    cosine = jnp.where(odd, s, c)
    sine = jnp.where(quadrant >= 2, -sine, sine)
    cosine = jnp.where((quadrant == 1) | (quadrant == 2), -cosine, cosine)
    return sine, cosine


def dot(a, b, dims):
    return lax.dot_general(a, b, (dims, ((), ())), preferred_element_type=F32)


def rotate_kernel(
    pos_hbm, freq_hbm, q_hbm, k_hbm, v_hbm, o_hbm,
    qr_ref, kr_ref, v_ref, o_ref, cos_ref, sin_ref, mine_ref, other_ref,
    pos_ref, freq_ref, q_ref, k_ref, small_sems, sems,
):
    keys_here = on_keys()
    small = [
        pltpu.make_async_copy(pos_hbm, pos_ref, small_sems.at[0]),
        pltpu.make_async_copy(freq_hbm, freq_ref, small_sems.at[1]),
    ]
    for copy in small:
        copy.start()
    pairs = ((k_hbm, k_ref), (v_hbm, v_ref), (q_hbm, q_ref), (o_hbm, o_ref))
    copies = [pltpu.make_async_copy(src, dst, sems.at[i]) for i, (src, dst) in enumerate(pairs)]
    for copy in copies[:2]:
        copy.start()
    first = lax.broadcasted_iota(jnp.int32, (HEAD_DIM, HEAD_DIM), 1) < HALF
    for copy in small:
        copy.wait()
    for copy in copies[2:]:
        copy.start()
    for i in range(BLOCK // HEAD_DIM):
        row = jnp.broadcast_to(pos_ref[i : i + 1, :].astype(F32), (HEAD_DIM, HEAD_DIM))
        sine, cosine = sin_cos(row.T * freq_ref[...])
        rows = slice(i * HEAD_DIM, (i + 1) * HEAD_DIM)
        cos_ref[rows, :] = cosine
        sin_ref[rows, :] = jnp.where(first, -sine, sine)

    def rotated(ref, out_ref, other_ref):
        states = []
        for h in range(HEADS):
            cols = slice(h * HEAD_DIM, (h + 1) * HEAD_DIM)
            a = ref[:, cols].astype(F32)
            rot = (a * cos_ref[...] + pltpu.roll(a, HALF, 1) * sin_ref[...]).astype(BF16)
            out_ref[:, cols] = rot
            states.append(dot(other_ref[:, cols], rot, ((0,), (0,))))
        return states

    for copy in copies[:2]:
        copy.wait()
    key_states = rotated(k_ref, kr_ref, v_ref)
    for h in range(HEADS):
        rows = slice(h * HEAD_DIM, (h + 1) * HEAD_DIM)
        mine_ref[rows, :] = key_states[h]
        other_ref[rows, :] = key_states[h]
    for copy in copies[2:]:
        copy.wait()
    query_states = rotated(q_ref, qr_ref, o_ref)
    for h in range(HEADS):
        rows = slice(h * HEAD_DIM, (h + 1) * HEAD_DIM)
        mine_ref[rows, :] = jnp.where(keys_here, mine_ref[rows, :], query_states[h])
        other_ref[rows, :] = jnp.where(keys_here, query_states[h], other_ref[rows, :])


FLIPPED = (18,)
ORDER = (
    [(18 + i) % 32 for i in range(32)],
    [(22 + i) % 32 for i in range(32)],
)
GROUPS = [[2 * p + (side ^ (p in FLIPPED)) for p in ORDER[side]] for side in range(2)]


def flipped():
    chip = lax.axis_index("stretch") // 2
    found = chip == FLIPPED[0]
    for p in FLIPPED[1:]:
        found = jnp.logical_or(found, chip == p)
    return found


def on_keys():
    return ((lax.axis_index("stretch") & 1) == 0) != flipped()


def triangle(a_ref, b_ref, c_ref, h, low):
    n = BLOCK // 2
    row = lax.broadcasted_iota(jnp.int32, (n, n), 0)
    col = lax.broadcasted_iota(jnp.int32, (n, n), 1)
    kept = row >= col if low else row <= col
    cols = slice(h * HEAD_DIM, (h + 1) * HEAD_DIM)
    halves = (slice(0, n), slice(n, BLOCK))

    def part(i, j):
        s = dot(a_ref[halves[i], cols], b_ref[halves[j], cols], ((1,), (1,)))
        if i == j:
            s = jnp.where(kept, s, 0.0)
        return dot(s.astype(BF16), c_ref[halves[j], cols], ((1,), (0,)))

    if low:
        return part(0, 0), part(1, 0) + part(1, 1)
    return part(0, 0) + part(0, 1), part(1, 1)


BESIDE_FIRST = (("dv", 0), ("dv", 1), ("dv", 2))
BESIDE_GROUPS = tuple(("dq", h) for h in range(HEADS)) + (("dv", 3),)
EXTRA = tuple(("dk", h) for h in range(HEADS))
Y_STEPS = (1, 3, 2)


def run_jobs(jobs, refs, out_ref):
    qr_ref, kr_ref, v_ref, o_ref = refs
    n = BLOCK // 2
    for i, (kind, h) in enumerate(jobs):
        cols = slice(i * HEAD_DIM, (i + 1) * HEAD_DIM)
        if kind == "dq":
            top, low = triangle(o_ref, v_ref, kr_ref, h, True)
        elif kind == "dk":
            top, low = triangle(v_ref, o_ref, qr_ref, h, False)
        else:
            top, low = triangle(kr_ref, qr_ref, o_ref, h, False)
        out_ref[:n, cols] = top
        out_ref[n:, cols] = low


def early():
    return lax.axis_index("stretch") < len(ORDER[0]) // 2


def first_kernel(*refs):
    run_jobs(BESIDE_FIRST, refs[:4], refs[4])

    @pl.when(early())
    def _():
        run_jobs(EXTRA, refs[:4], refs[5])


def groups_kernel(*refs):
    run_jobs(BESIDE_GROUPS, refs[:4], refs[5])


def last_kernel(*refs):
    @pl.when(jnp.logical_not(early()))
    def _():
        run_jobs(EXTRA, refs[:4], refs[5])


def scan_kernel(r_ref, total_ref, pre_ref):
    n = r_ref.shape[0]
    before, after = (sorted(range(n), key=lambda i: order[i]) for order in ORDER)
    total = r_ref[0]
    for i in range(1, n):
        total = total + r_ref[i]
    total_ref[...] = total
    up = on_keys()

    @pl.when(up)
    def _():
        acc = jnp.zeros_like(total)
        for i in before:
            pre_ref[i] = acc
            acc = acc + r_ref[i]

    @pl.when(jnp.logical_not(up))
    def _():
        acc = jnp.zeros_like(total)
        for i in reversed(after):
            pre_ref[i] = acc
            acc = acc + r_ref[i]


def pair_kernel(mine_ref, came_ref, _, out_ref):
    out_ref[...] = mine_ref[...] + came_ref[...]


def own_state_kernel(chip_ref, mine_ref, came_ref, own_ref, sent_ref):
    turned = flipped()
    own_ref[...] = chip_ref[...] + jnp.where(turned, came_ref[...], 0.0)
    sent_ref[...] = chip_ref[...] + jnp.where(turned, 0.0, mine_ref[...])


def place_kernel(pre_ref, a_ref, b_ref, c_ref, _, out_ref):
    above = jnp.zeros(a_ref.shape, F32)
    up, y = on_keys(), lax.axis_index("grp")
    for step, ref in zip(Y_STEPS, (a_ref, b_ref, c_ref)):
        below = (y ^ step) < y
        above = above + jnp.where(up == below, ref[...], 0.0)
    out_ref[...] = pre_ref[...] + above[None]


def write_gradients(kinds, prior, later, refs, *, scale):
    kr_ref, v_ref, o_ref, cos_ref, sin_ref, first_ref, groups_ref, soon_ref, late_ref, outs, held, sems = refs
    copies = []

    def intra(kind, h):
        for ref, jobs in ((first_ref, BESIDE_FIRST), (groups_ref, BESIDE_GROUPS)):
            if (kind, h) in jobs:
                i = jobs.index((kind, h))
                return ref[:, i * HEAD_DIM : (i + 1) * HEAD_DIM]
        i = EXTRA.index((kind, h))
        cols = slice(i * HEAD_DIM, (i + 1) * HEAD_DIM)
        return jnp.where(early(), soon_ref[:, cols], late_ref[:, cols])

    cosine = cos_ref[...] * scale
    sine = sin_ref[...] * scale
    for h in range(HEADS):
        cols = slice(h * HEAD_DIM, (h + 1) * HEAD_DIM)
        for kind in kinds:
            if kind == "dv":
                state = later[cols, :].astype(BF16)
                grad = (intra(kind, h) + dot(kr_ref[:, cols], state, ((1,), (1,)))) * scale
            else:
                rows_ref, state = (o_ref, prior) if kind == "dq" else (v_ref, later)
                grad = intra(kind, h) + dot(rows_ref[:, cols], state[cols, :].astype(BF16), ((1,), (0,)))
                grad = grad * cosine - pltpu.roll(grad, HALF, 1) * sine
            place = KINDS.index(kind)
            held[place][:, cols] = grad.astype(BF16)
            copy = pltpu.make_async_copy(held[place].at[:, cols], outs[place].at[:, cols], sems.at[len(copies)])
            copy.start()
            copies.append(copy)
    for copy in copies:
        copy.wait()


KINDS = ("dq", "dk", "dv")


def own_kernel(chip_ref, *refs, scale):
    refs = (*refs[:9], refs[9:12], refs[12:15], refs[15])
    keys_here = on_keys()

    @pl.when(keys_here)
    def _():
        write_gradients(("dq",), chip_ref, None, refs, scale=scale)

    @pl.when(jnp.logical_not(keys_here))
    def _():
        write_gradients(("dk", "dv"), None, chip_ref, refs, scale=scale)


def final_kernel(came_ref, *refs, scale):
    refs = (*refs[:9], refs[12:15], refs[15:18], refs[18])
    keys_here = on_keys()

    @pl.when(keys_here)
    def _():
        write_gradients(("dk", "dv"), None, came_ref, refs, scale=scale)

    @pl.when(jnp.logical_not(keys_here))
    def _():
        write_gradients(("dq",), came_ref, None, refs, scale=scale)


def call(kernel, outs, in_specs, cost, out_spec=WHOLE, scratch=(), aliases=None):
    return pl.pallas_call(
        kernel,
        out_shape=tuple(jax.ShapeDtypeStruct(s, d) for s, d in outs),
        in_specs=in_specs,
        out_specs=tuple(out_spec for _ in outs),
        scratch_shapes=scratch,
        input_output_aliases=aliases or {},
        compiler_params=params(),
        cost_estimate=pl.CostEstimate(flops=cost[0], bytes_accessed=cost[1], transcendentals=0),
    )


def shards(queries, keys, values, grad_out, positions):
    ny = lax.axis_size("grp")
    scale = 1.0 / math.sqrt(HEAD_DIM * BLOCK * ny * lax.axis_size("stretch"))
    wide, state, table = (BLOCK, WIDTH), (WIDTH, HEAD_DIM), (BLOCK, HEAD_DIM)
    groups = BLOCK // HEAD_DIM
    qr, kr, v, o, cosine, sine, mine, other = call(
        rotate_kernel,
        [(wide, BF16)] * 4 + [(table, F32)] * 2 + [(state, F32)] * 2,
        [HBM] * 6,
        (2 * 8 * 512 * 128 * 128, 4 << 20),
        scratch=[
            pltpu.VMEM((groups, HEAD_DIM), jnp.int32),
            pltpu.VMEM((1, HEAD_DIM), F32),
            pltpu.VMEM(wide, BF16),
            pltpu.VMEM(wide, BF16),
            pltpu.SemaphoreType.DMA((2,)),
            pltpu.SemaphoreType.DMA((4,)),
        ],
    )(*[
        pltpu.with_memory_space_constraint(a, pltpu.HBM)
        for a in (positions.reshape(groups, HEAD_DIM), jnp.asarray(FREQUENCY), queries, keys, values, grad_out)
    ])

    def work(*jobs):
        return (2 * sum(map(len, jobs)) * 2 * BLOCK * BLOCK * HEAD_DIM, 3 << 20)

    def products(*jobs):
        return [((BLOCK, len(each) * HEAD_DIM), F32) for each in jobs]

    swap = [(i, i ^ 1) for i in range(2 * len(ORDER[0]))]
    chips = len(ORDER[0])
    piece = (WIDTH // chips, HEAD_DIM)
    came = lax.ppermute(other, "stretch", swap)
    rows = (qr, kr, v, o)
    first, soon = call(
        first_kernel, products(BESIDE_FIRST, EXTRA), [WHOLE] * 4, work(BESIDE_FIRST)
    )(*rows)
    (pair,) = call(pair_kernel, [(state, F32)], [WHOLE] * 3, (0, 1 << 19))(mine, came, first)
    pieces = lax.all_to_all(pair.reshape((chips,) + piece), "stretch", 0, 0, axis_index_groups=GROUPS)
    total, pre = call(
        scan_kernel, [(piece, F32), ((chips,) + piece, F32)], [WHOLE], (0, 1 << 19)
    )(pieces)
    (groups,) = call(
        groups_kernel, products(BESIDE_GROUPS), [WHOLE] * 5, work(BESIDE_GROUPS)
    )(*rows, total)
    others = [lax.ppermute(total, "grp", [(i, i ^ step) for i in range(ny)]) for step in Y_STEPS]
    (place,) = call(
        place_kernel, [((chips,) + piece, F32)], [WHOLE] * 5, (0, 1 << 19)
    )(pre, *others, groups)
    chip = lax.all_to_all(place, "stretch", 0, 0, axis_index_groups=GROUPS).reshape(state)
    own_state, sent = call(own_state_kernel, [(state, F32)] * 2, [WHOLE] * 3, (0, 1 << 19))(chip, mine, came)
    came = lax.ppermute(sent, "stretch", swap)
    (late,) = call(
        last_kernel, products(EXTRA), [WHOLE] * 5, work(EXTRA)
    )(*rows, chip)

    def own(*refs):
        own_kernel(*refs, scale=scale)

    def final(*refs):
        final_kernel(*refs, scale=scale)

    held = [pltpu.VMEM(wide, BF16)] * 3 + [pltpu.SemaphoreType.DMA((2 * HEADS,))]
    common = (kr, v, o, cosine, sine, first, groups, soon, late)
    cost = (2 * 4 * 2 * 512 * 128 * 128, 4 << 20)
    begun = call(own, [(wide, BF16)] * 3, [WHOLE] * 10, cost, out_spec=HBM, scratch=held)(own_state, *common)
    return call(
        final, [(wide, BF16)] * 3, [WHOLE] * 10 + [HBM] * 3, cost, out_spec=HBM, scratch=held,
        aliases={10: 0, 11: 1, 12: 2},
    )(came, *common, *begun)


def solution(mesh):
    every = ("grp", "stretch")
    return jax.shard_map(
        shards,
        mesh=mesh,
        in_specs=(P(every, None),) * 4 + (P(every),),
        out_specs=(P(every, None),) * 3,
        check_vma=False,
    )
```

```python
import math

import numpy as np
import jax
import jax.numpy as jnp
from jax import lax
from jax.experimental import pallas as pl
from jax.experimental.pallas import tpu as pltpu
from jax.sharding import PartitionSpec as P

HEADS = 4
HEAD_DIM = 128
BLOCK = 512
THETA = 500000.0
WIDTH = HEADS * HEAD_DIM
HALF = HEAD_DIM // 2
F32 = jnp.float32
BF16 = jnp.bfloat16
VMEM_LIMIT = 16 * 1024 * 1024
WHOLE = pl.BlockSpec(memory_space=pltpu.VMEM)
HBM = pl.BlockSpec(memory_space=pltpu.HBM)

FREQUENCY = np.tile(
    np.power(THETA, -2.0 * np.arange(HALF) / HEAD_DIM), 2
).astype(np.float32)[None, :]

HALF_PI = (1.5703125, 4.837512969970703125e-4, 7.54978995489188216e-8)


def params():
    return pltpu.CompilerParams(vmem_limit_bytes=VMEM_LIMIT)


def sin_cos(angle):
    turns = jnp.floor(angle * (2.0 / math.pi) + 0.5)
    r = angle - turns * HALF_PI[0]
    r = r - turns * HALF_PI[1]
    r = r - turns * HALF_PI[2]
    r2 = r * r
    s = r + r * r2 * (-1.6666654611e-1 + r2 * (8.3321608736e-3 + r2 * -1.9515295891e-4))
    c = 1.0 + r2 * (-0.5 + r2 * (4.166664568298827e-2 + r2 * (-1.388731625493765e-3 + r2 * 2.443315711809948e-5)))
    quadrant = turns.astype(jnp.int32) & 3
    odd = (quadrant & 1) == 1
    sine = jnp.where(odd, c, s)
    cosine = jnp.where(odd, s, c)
    sine = jnp.where(quadrant >= 2, -sine, sine)
    cosine = jnp.where((quadrant == 1) | (quadrant == 2), -cosine, cosine)
    return sine, cosine


def dot(a, b, dims):
    return lax.dot_general(a, b, (dims, ((), ())), preferred_element_type=F32)


def rotate_kernel(
    pos_hbm, freq_hbm, q_hbm, k_hbm, v_hbm, o_hbm,
    qr_ref, kr_ref, v_ref, o_ref, cos_ref, sin_ref, mine_ref, other_ref,
    pos_ref, freq_ref, q_ref, k_ref, small_sems, sems,
):
    keys_here = on_keys()
    small = [
        pltpu.make_async_copy(pos_hbm, pos_ref, small_sems.at[0]),
        pltpu.make_async_copy(freq_hbm, freq_ref, small_sems.at[1]),
    ]
    for copy in small:
        copy.start()
    pairs = ((k_hbm, k_ref), (v_hbm, v_ref), (q_hbm, q_ref), (o_hbm, o_ref))
    copies = [pltpu.make_async_copy(src, dst, sems.at[i]) for i, (src, dst) in enumerate(pairs)]
    for copy in copies[:2]:
        copy.start()
    first = lax.broadcasted_iota(jnp.int32, (HEAD_DIM, HEAD_DIM), 1) < HALF
    for copy in small:
        copy.wait()
    for copy in copies[2:]:
        copy.start()
    for i in range(BLOCK // HEAD_DIM):
        row = jnp.broadcast_to(pos_ref[i : i + 1, :].astype(F32), (HEAD_DIM, HEAD_DIM))
        sine, cosine = sin_cos(row.T * freq_ref[...])
        rows = slice(i * HEAD_DIM, (i + 1) * HEAD_DIM)
        cos_ref[rows, :] = cosine
        sin_ref[rows, :] = jnp.where(first, -sine, sine)

    def rotated(ref, out_ref, other_ref):
        states = []
        for h in range(HEADS):
            cols = slice(h * HEAD_DIM, (h + 1) * HEAD_DIM)
            a = ref[:, cols].astype(F32)
            rot = (a * cos_ref[...] + pltpu.roll(a, HALF, 1) * sin_ref[...]).astype(BF16)
            out_ref[:, cols] = rot
            states.append(dot(other_ref[:, cols], rot, ((0,), (0,))))
        return states

    for copy in copies[:2]:
        copy.wait()
    key_states = rotated(k_ref, kr_ref, v_ref)
    for h in range(HEADS):
        rows = slice(h * HEAD_DIM, (h + 1) * HEAD_DIM)
        mine_ref[rows, :] = key_states[h]
        other_ref[rows, :] = key_states[h]
    for copy in copies[2:]:
        copy.wait()
    query_states = rotated(q_ref, qr_ref, o_ref)
    for h in range(HEADS):
        rows = slice(h * HEAD_DIM, (h + 1) * HEAD_DIM)
        mine_ref[rows, :] = jnp.where(keys_here, mine_ref[rows, :], query_states[h])
        other_ref[rows, :] = jnp.where(keys_here, query_states[h], other_ref[rows, :])


FLIPPED = (18,)
ORDER = (
    [(18 + i) % 32 for i in range(32)],
    [(22 + i) % 32 for i in range(32)],
)
GROUPS = [[2 * p + (side ^ (p in FLIPPED)) for p in ORDER[side]] for side in range(2)]


def flipped():
    chip = lax.axis_index("stretch") // 2
    found = chip == FLIPPED[0]
    for p in FLIPPED[1:]:
        found = jnp.logical_or(found, chip == p)
    return found


def on_keys():
    return ((lax.axis_index("stretch") & 1) == 0) != flipped()


def triangle(a_ref, b_ref, c_ref, h, low):
    n = BLOCK // 2
    row = lax.broadcasted_iota(jnp.int32, (n, n), 0)
    col = lax.broadcasted_iota(jnp.int32, (n, n), 1)
    kept = row >= col if low else row <= col
    cols = slice(h * HEAD_DIM, (h + 1) * HEAD_DIM)
    halves = (slice(0, n), slice(n, BLOCK))

    def part(i, j):
        s = dot(a_ref[halves[i], cols], b_ref[halves[j], cols], ((1,), (1,)))
        if i == j:
            s = jnp.where(kept, s, 0.0)
        return dot(s.astype(BF16), c_ref[halves[j], cols], ((1,), (0,)))

    if low:
        return part(0, 0), part(1, 0) + part(1, 1)
    return part(0, 0) + part(0, 1), part(1, 1)


BESIDE_FIRST = (("dv", 0), ("dv", 1), ("dv", 2))
BESIDE_GROUPS = tuple(("dq", h) for h in range(HEADS)) + (("dv", 3),)
EXTRA = tuple(("dk", h) for h in range(HEADS))
Y_STEPS = (1, 3, 2)


def run_jobs(jobs, refs, out_ref):
    qr_ref, kr_ref, v_ref, o_ref = refs
    n = BLOCK // 2
    for i, (kind, h) in enumerate(jobs):
        cols = slice(i * HEAD_DIM, (i + 1) * HEAD_DIM)
        if kind == "dq":
            top, low = triangle(o_ref, v_ref, kr_ref, h, True)
        elif kind == "dk":
            top, low = triangle(v_ref, o_ref, qr_ref, h, False)
        else:
            top, low = triangle(kr_ref, qr_ref, o_ref, h, False)
        out_ref[:n, cols] = top
        out_ref[n:, cols] = low


def early():
    return jnp.logical_or(lax.axis_index("stretch") < len(ORDER[0]) // 2, lax.axis_index("grp") == 0)


def first_kernel(*refs):
    run_jobs(BESIDE_FIRST, refs[:4], refs[4])

    @pl.when(early())
    def _():
        run_jobs(EXTRA, refs[:4], refs[5])


def groups_kernel(*refs):
    run_jobs(BESIDE_GROUPS, refs[:4], refs[5])


def last_kernel(*refs):
    @pl.when(jnp.logical_not(early()))
    def _():
        run_jobs(EXTRA, refs[:4], refs[5])


def scan_kernel(r_ref, total_ref, pre_ref):
    n = r_ref.shape[0]
    before, after = (sorted(range(n), key=lambda i: order[i]) for order in ORDER)
    total = r_ref[0]
    for i in range(1, n):
        total = total + r_ref[i]
    total_ref[...] = total
    up = on_keys()

    @pl.when(up)
    def _():
        acc = jnp.zeros_like(total)
        for i in before:
            pre_ref[i] = acc
            acc = acc + r_ref[i]

    @pl.when(jnp.logical_not(up))
    def _():
        acc = jnp.zeros_like(total)
        for i in reversed(after):
            pre_ref[i] = acc
            acc = acc + r_ref[i]


def pair_kernel(mine_ref, came_ref, _, out_ref):
    out_ref[...] = mine_ref[...] + came_ref[...]


def own_state_kernel(chip_ref, mine_ref, came_ref, own_ref, sent_ref):
    turned = flipped()
    own_ref[...] = chip_ref[...] + jnp.where(turned, came_ref[...], 0.0)
    sent_ref[...] = chip_ref[...] + jnp.where(turned, 0.0, mine_ref[...])


def place_kernel(pre_ref, a_ref, b_ref, c_ref, _, out_ref):
    above = jnp.zeros(a_ref.shape, F32)
    up, y = on_keys(), lax.axis_index("grp")
    for step, ref in zip(Y_STEPS, (a_ref, b_ref, c_ref)):
        below = (y ^ step) < y
        above = above + jnp.where(up == below, ref[...], 0.0)
    out_ref[...] = pre_ref[...] + above[None]


def write_gradients(kinds, prior, later, refs, *, scale):
    kr_ref, v_ref, o_ref, cos_ref, sin_ref, first_ref, groups_ref, soon_ref, late_ref, outs, held, sems = refs
    copies = []

    def intra(kind, h):
        for ref, jobs in ((first_ref, BESIDE_FIRST), (groups_ref, BESIDE_GROUPS)):
            if (kind, h) in jobs:
                i = jobs.index((kind, h))
                return ref[:, i * HEAD_DIM : (i + 1) * HEAD_DIM]
        i = EXTRA.index((kind, h))
        cols = slice(i * HEAD_DIM, (i + 1) * HEAD_DIM)
        return jnp.where(early(), soon_ref[:, cols], late_ref[:, cols])

    cosine = cos_ref[...] * scale
    sine = sin_ref[...] * scale
    for h in range(HEADS):
        cols = slice(h * HEAD_DIM, (h + 1) * HEAD_DIM)
        for kind in kinds:
            if kind == "dv":
                state = later[cols, :].astype(BF16)
                grad = (intra(kind, h) + dot(kr_ref[:, cols], state, ((1,), (1,)))) * scale
            else:
                rows_ref, state = (o_ref, prior) if kind == "dq" else (v_ref, later)
                grad = intra(kind, h) + dot(rows_ref[:, cols], state[cols, :].astype(BF16), ((1,), (0,)))
                grad = grad * cosine - pltpu.roll(grad, HALF, 1) * sine
            place = KINDS.index(kind)
            held[place][:, cols] = grad.astype(BF16)
            copy = pltpu.make_async_copy(held[place].at[:, cols], outs[place].at[:, cols], sems.at[len(copies)])
            copy.start()
            copies.append(copy)
    for copy in copies:
        copy.wait()


KINDS = ("dq", "dk", "dv")


def own_kernel(chip_ref, *refs, scale):
    refs = (*refs[:9], refs[9:12], refs[12:15], refs[15])
    keys_here = on_keys()

    @pl.when(keys_here)
    def _():
        write_gradients(("dq",), chip_ref, None, refs, scale=scale)

    @pl.when(jnp.logical_not(keys_here))
    def _():
        write_gradients(("dk", "dv"), None, chip_ref, refs, scale=scale)


def final_kernel(came_ref, *refs, scale):
    refs = (*refs[:9], refs[12:15], refs[15:18], refs[18])
    keys_here = on_keys()

    @pl.when(keys_here)
    def _():
        write_gradients(("dk", "dv"), None, came_ref, refs, scale=scale)

    @pl.when(jnp.logical_not(keys_here))
    def _():
        write_gradients(("dq",), came_ref, None, refs, scale=scale)


def call(kernel, outs, in_specs, cost, out_spec=WHOLE, scratch=(), aliases=None):
    return pl.pallas_call(
        kernel,
        out_shape=tuple(jax.ShapeDtypeStruct(s, d) for s, d in outs),
        in_specs=in_specs,
        out_specs=tuple(out_spec for _ in outs),
        scratch_shapes=scratch,
        input_output_aliases=aliases or {},
        compiler_params=params(),
        cost_estimate=pl.CostEstimate(flops=cost[0], bytes_accessed=cost[1], transcendentals=0),
    )


def shards(queries, keys, values, grad_out, positions):
    ny = lax.axis_size("grp")
    scale = 1.0 / math.sqrt(HEAD_DIM * BLOCK * ny * lax.axis_size("stretch"))
    wide, state, table = (BLOCK, WIDTH), (WIDTH, HEAD_DIM), (BLOCK, HEAD_DIM)
    groups = BLOCK // HEAD_DIM
    qr, kr, v, o, cosine, sine, mine, other = call(
        rotate_kernel,
        [(wide, BF16)] * 4 + [(table, F32)] * 2 + [(state, F32)] * 2,
        [HBM] * 6,
        (2 * 8 * 512 * 128 * 128, 4 << 20),
        scratch=[
            pltpu.VMEM((groups, HEAD_DIM), jnp.int32),
            pltpu.VMEM((1, HEAD_DIM), F32),
            pltpu.VMEM(wide, BF16),
            pltpu.VMEM(wide, BF16),
            pltpu.SemaphoreType.DMA((2,)),
            pltpu.SemaphoreType.DMA((4,)),
        ],
    )(*[
        pltpu.with_memory_space_constraint(a, pltpu.HBM)
        for a in (positions.reshape(groups, HEAD_DIM), jnp.asarray(FREQUENCY), queries, keys, values, grad_out)
    ])

    def work(*jobs):
        return (2 * sum(map(len, jobs)) * 2 * BLOCK * BLOCK * HEAD_DIM, 3 << 20)

    def products(*jobs):
        return [((BLOCK, len(each) * HEAD_DIM), F32) for each in jobs]

    swap = [(i, i ^ 1) for i in range(2 * len(ORDER[0]))]
    chips = len(ORDER[0])
    piece = (WIDTH // chips, HEAD_DIM)
    came = lax.ppermute(other, "stretch", swap)
    rows = (qr, kr, v, o)
    first, soon = call(
        first_kernel, products(BESIDE_FIRST, EXTRA), [WHOLE] * 4, work(BESIDE_FIRST)
    )(*rows)
    (pair,) = call(pair_kernel, [(state, F32)], [WHOLE] * 3, (0, 1 << 19))(mine, came, first)
    pieces = lax.all_to_all(pair.reshape((chips,) + piece), "stretch", 0, 0, axis_index_groups=GROUPS)
    total, pre = call(
        scan_kernel, [(piece, F32), ((chips,) + piece, F32)], [WHOLE], (0, 1 << 19)
    )(pieces)
    (groups,) = call(
        groups_kernel, products(BESIDE_GROUPS), [WHOLE] * 5, work(BESIDE_GROUPS)
    )(*rows, total)
    others = [lax.ppermute(total, "grp", [(i, i ^ step) for i in range(ny)]) for step in Y_STEPS]
    (place,) = call(
        place_kernel, [((chips,) + piece, F32)], [WHOLE] * 5, (0, 1 << 19)
    )(pre, *others, groups)
    chip = lax.all_to_all(place, "stretch", 0, 0, axis_index_groups=GROUPS).reshape(state)
    own_state, sent = call(own_state_kernel, [(state, F32)] * 2, [WHOLE] * 3, (0, 1 << 19))(chip, mine, came)
    came = lax.ppermute(sent, "stretch", swap)
    (late,) = call(
        last_kernel, products(EXTRA), [WHOLE] * 5, work(EXTRA)
    )(*rows, chip)

    def own(*refs):
        own_kernel(*refs, scale=scale)

    def final(*refs):
        final_kernel(*refs, scale=scale)

    held = [pltpu.VMEM(wide, BF16)] * 3 + [pltpu.SemaphoreType.DMA((2 * HEADS,))]
    common = (kr, v, o, cosine, sine, first, groups, soon, late)
    cost = (2 * 4 * 2 * 512 * 128 * 128, 4 << 20)
    begun = call(own, [(wide, BF16)] * 3, [WHOLE] * 10, cost, out_spec=HBM, scratch=held)(own_state, *common)
    return call(
        final, [(wide, BF16)] * 3, [WHOLE] * 10 + [HBM] * 3, cost, out_spec=HBM, scratch=held,
        aliases={10: 0, 11: 1, 12: 2},
    )(came, *common, *begun)


def solution(mesh):
    every = ("grp", "stretch")
    return jax.shard_map(
        shards,
        mesh=mesh,
        in_specs=(P(every, None),) * 4 + (P(every),),
        out_specs=(P(every, None),) * 3,
        check_vma=False,
    )
```
